32 devices in a mesh: group: 2 (over y), seq: 8 (over z, x), tp: 2 (over core).
Axes of the slice: x: 2, y: 2, z: 4, core: 2. Of those that a mesh axis runs over, the one named last changes fastest.
Arguments:
- hidden: bfloat16 [4096, 7168], P(('group', 'seq', 'tp')), parts along dimension 0, may hold values from -6 to 6
- in_gain: bfloat16 [7168], replicated, may hold values from 0.099609375 to 1.8984375
- kv_weight: bfloat16 [7168, 576], P('seq', 'tp'), may hold values from -0.0625 to 0.0625
- kv_gain: bfloat16 [512], replicated, may hold values from 0.099609375 to 1.8984375
- block_owner: int32 [32], replicated, may hold values from 0 to 7, as said below
- block_slot: int32 [32], replicated, may hold values from 0 to 7, as said below
Outputs:
- owner_cache: bfloat16 [128, 64, 576], P(('group', 'seq'), None, 'tp'), parts along dimension 0
- owner_scales: bfloat16 [128, 64], P(('group', 'seq')), parts along dimension 0
The draws below stay inside these ranges and needn't reach their ends.
There are 2 independent parts, one for each index of `group`. The reference program is written for one: setup_inputs(seed, part) draws one part's arguments, and reference() takes and returns one part's arrays. A program takes and returns all parts, laid end to end along the dimension named above; an argument that names none is the same for every part. Nothing has to cross between parts.
Inputs may be any that keep to these rules, and one draw needn't show every extreme that they name: `block_owner`: each owner is named by 0 or 2 of the 4 blocks of one index of seq, so at most 2 from one device; every owner receives at most 8 blocks, and some owner exactly that many; loads are uneven. `block_slot`: the slots named for one owner are distinct.
All inputs are finite; a program needn't handle non-finite values. Where the reference program divides by a largest or mean magnitude, that divisor is 1e-20 or more.
Results may differ from the reference program's by a relative error of at most 0.0085.
Values may be sent and summed in bfloat16 or wider, within the bound.
A program may use at most 128 MiB of HBM per device.

```python
import math
import jax
import jax.numpy as jnp
import numpy as np
from jax import lax

D = 7168
LAT = 512
ROPE = 64
TOK_DEV = 256
KVW = 576
BLK_DEV = 4
SLOTS = 8
TOKENS = 2048
NBLK = 32
N_SEQ = 8


def block_tables(key):
    key = jax.random.fold_in(key, 11)
    pair_count = BLK_DEV // 2
    quarter = N_SEQ // 4
    pattern = np.concatenate([np.full(quarter, 2 * pair_count), np.full(quarter, pair_count), np.full(N_SEQ - 2 * quarter, pair_count // 2)]).astype(np.int64)
    sorted_labels = np.repeat(np.arange(N_SEQ), pattern)
    key_label, key_rows, key_shuffle, key_slots = jax.random.split(key, 4)
    labels = jax.random.permutation(key_label, N_SEQ)
    position_owner = labels[jnp.asarray(sorted_labels, dtype=jnp.int32)]
    owner_grid = position_owner.reshape(pair_count, N_SEQ).T
    owner_grid = owner_grid[jax.random.permutation(key_rows, N_SEQ)]
    doubled = jnp.repeat(owner_grid, 2, axis=1)
    shuffles = jax.vmap(lambda one_key: jax.random.permutation(one_key, BLK_DEV))(jax.random.split(key_shuffle, N_SEQ))
    owner = jnp.take_along_axis(doubled, shuffles, axis=1).reshape(-1).astype(jnp.int32)
    one_hot = (owner[:, None] == jnp.arange(N_SEQ, dtype=jnp.int32)[None, :]).astype(jnp.int32)
    running = jnp.cumsum(one_hot, axis=0) - one_hot
    owner_rank = jnp.sum(running * one_hot, axis=1)
    slot_table = jax.vmap(lambda one_key: jax.random.permutation(one_key, SLOTS))(jax.random.split(key_slots, N_SEQ))
    slot = slot_table[owner, owner_rank].astype(jnp.int32)
    return (owner, slot)


def draw_block_owner(key, part):
    owner, slot = block_tables(key)
    return owner


def draw_block_slot(key, part):
    owner, slot = block_tables(key)
    return slot


def steps_of(stream_key, extent, cuts, low, high):
    def one(position, blocks):
        draws = jax.random.uniform(jax.random.fold_in(jax.random.fold_in(stream_key, 6), position), (blocks,), jnp.float32, low / len(cuts), high / len(cuts))
        return jnp.repeat(jnp.exp(draws), extent[position] // blocks).reshape((-1,) + (1,) * (len(extent) - position - 1))

    loudness = one(*cuts[0])
    for cut in cuts[1:]:
        loudness = loudness * one(*cut)
    return loudness


def bell_draw(own_key, dims, spread, limit, cuts=(), held_as=jnp.bfloat16):
    loudness = steps_of(own_key, dims, cuts, -0.22, 0.18) if cuts else 1.0
    result = jax.random.normal(own_key, dims, jnp.float32) * spread * loudness
    return jnp.minimum(jnp.maximum(result, -limit), limit).astype(held_as)


def setup_inputs(seed: int = 0, part: int = 0) -> dict:
    key_of = jax.random.split(jax.random.key(seed), 7)
    own_keys = jax.random.split(jax.random.fold_in(key_of[6], part), 7)
    hidden = bell_draw(own_keys[0], (TOKENS, D), 1.0, 6.0, ((0, 16),))
    in_gain = jnp.clip(1.0 + 0.18 * jax.random.normal(key_of[1], (D,), jnp.float32), 0.099609375, 1.8984375).astype(jnp.bfloat16)
    kv_weight = bell_draw(key_of[2], (D, KVW), D ** -0.5, 0.0625, ((0, 8), (1, 2)))
    kv_gain = jnp.clip(1.0 + 0.18 * jax.random.normal(key_of[3], (LAT,), jnp.float32), 0.099609375, 1.8984375).astype(jnp.bfloat16)
    block_owner = draw_block_owner(jax.random.fold_in(key_of[6], 71), part)
    block_slot = draw_block_slot(jax.random.fold_in(key_of[6], 71), part)
    return dict(hidden=hidden, in_gain=in_gain, kv_weight=kv_weight, kv_gain=kv_gain, block_owner=block_owner, block_slot=block_slot)


EPSILON = 1e-06

def rope_periods(rope_width):
    return np.floor(2.0 * np.pi * 10000.0 ** (np.arange(rope_width // 2) * 2.0 / rope_width) + 0.5).astype(np.int32)

def normalize(values, in_gain):
    wide = values.astype(jnp.float32)
    power = lax.optimization_barrier(jnp.mean(wide * wide, axis=1, keepdims=True))
    return (wide * lax.rsqrt(power + EPSILON) * in_gain.astype(jnp.float32)).astype(jnp.bfloat16)

def shape_latent(projected, power, gain_cols, positions, col_index):
    scaled = projected * lax.rsqrt(power / LAT + EPSILON)[:, None] * gain_cols[None, :]
    periods = jnp.asarray(rope_periods(ROPE))
    phase = (positions[:, None] % periods[None, :]).astype(jnp.float32) * (2.0 * math.pi) / periods.astype(jnp.float32)
    cosine = jnp.cos(phase)
    sine = jnp.sin(phase)
    col_total = projected.shape[1]
    rope_tail = projected[:, col_total - ROPE:]
    lower_half = rope_tail[:, :ROPE // 2]
    upper_half = rope_tail[:, ROPE // 2:]
    rotated = jnp.concatenate([lower_half * cosine - upper_half * sine, upper_half * cosine + lower_half * sine], axis=1)
    rotated_full = jnp.concatenate([projected[:, :col_total - ROPE], rotated], axis=1)
    return jnp.where((col_index >= LAT)[None, :], rotated_full, scaled)

def reference(hidden, in_gain, kv_weight, kv_gain, block_owner, block_slot):
    gain_cols = jnp.concatenate([kv_gain.astype(jnp.float32), jnp.ones((ROPE,), jnp.float32)])
    col_index = jnp.arange(KVW, dtype=jnp.int32)

    def one_shard(shard_index):
        shard_rows = lax.dynamic_slice_in_dim(hidden, shard_index * TOK_DEV, TOK_DEV, 0)
        normed = normalize(shard_rows, in_gain)
        projected = jnp.dot(normed, kv_weight, preferred_element_type=jnp.float32)
        power = lax.optimization_barrier(jnp.sum(projected[:, :LAT] * projected[:, :LAT], axis=1))
        positions = shard_index * TOK_DEV + jnp.arange(TOK_DEV, dtype=jnp.int32)
        shaped = shape_latent(projected, power, gain_cols, positions, col_index)
        token_scale = (lax.optimization_barrier(jnp.max(jnp.abs(shaped), axis=1)) + EPSILON).astype(jnp.bfloat16)
        quant = (shaped / token_scale.astype(jnp.float32)[:, None]).astype(jnp.bfloat16)
        return (quant, token_scale)
    quant, token_scale = lax.map(one_shard, jnp.arange(N_SEQ, dtype=jnp.int32))
    blocks = quant.reshape(NBLK, 64, KVW)
    block_scales = token_scale.reshape(NBLK, 64)
    target = (block_owner * SLOTS + block_slot).astype(jnp.int32)
    owner_cache = jnp.zeros((N_SEQ * SLOTS, 64, KVW), jnp.bfloat16).at[target].set(blocks)
    owner_scales = jnp.zeros((N_SEQ * SLOTS, 64), jnp.bfloat16).at[target].set(block_scales)
    return (owner_cache, owner_scales)
```

```python
import functools
import math

import jax
import jax.numpy as jnp
import numpy as np
from jax import lax
from jax.experimental import pallas as pl
from jax.experimental.pallas import tpu as pltpu
from jax.sharding import PartitionSpec as P

LAT = 512
ROPE = 64
SEND_CAP = 2


EPSILON = 1e-06


def rope_periods(rope_width):
    return np.floor(
        2.0 * np.pi * 10000.0 ** (np.arange(rope_width // 2) * 2.0 / rope_width) + 0.5
    ).astype(np.int32)


def normalize(values, in_gain):
    wide = values.astype(jnp.float32)
    power = jnp.mean(wide * wide, axis=1, keepdims=True)
    return (wide * lax.rsqrt(power + EPSILON) * in_gain.astype(jnp.float32)).astype(jnp.bfloat16)


def shape_latent(projected, power, gain_cols, positions, col_index):
    scaled = projected * lax.rsqrt(power / LAT + EPSILON)[:, None] * gain_cols[None, :]
    periods = jnp.asarray(rope_periods(ROPE))
    phase = (
        (positions[:, None] % periods[None, :]).astype(jnp.float32)
        * (2.0 * math.pi)
        / periods.astype(jnp.float32)
    )
    cosine = jnp.cos(phase)
    sine = jnp.sin(phase)
    col_total = projected.shape[1]
    rope_tail = projected[:, col_total - ROPE :]
    lower_half = rope_tail[:, : ROPE // 2]
    upper_half = rope_tail[:, ROPE // 2 :]
    rotated = jnp.concatenate(
        [lower_half * cosine - upper_half * sine, upper_half * cosine + lower_half * sine], axis=1
    )
    rotated_full = jnp.concatenate([projected[:, : col_total - ROPE], rotated], axis=1)
    return jnp.where((col_index >= LAT)[None, :], rotated_full, scaled)


def hand_off(quant, token_scale, block_owner, block_slot):
    seq_count = lax.axis_size("seq")
    seq_index = lax.axis_index("seq")
    block_count = quant.shape[0] // 64
    col_width = quant.shape[1]
    blocks_flat = quant.reshape(block_count, 64 * col_width)
    scales_flat = token_scale.reshape(block_count, 64)
    owner_grid = block_owner.reshape(seq_count, block_count)
    slot_grid = block_slot.reshape(seq_count, block_count)
    earlier = (jnp.arange(block_count)[:, None] < jnp.arange(block_count)[None, :]).astype(
        jnp.int32
    )
    own_row = lax.dynamic_slice_in_dim(owner_grid, seq_index, 1, 0)[0]
    same_owner = (own_row[:, None] == own_row[None, :]).astype(jnp.int32)
    send_rank = jnp.sum(same_owner * earlier, axis=0)
    targets = jnp.arange(seq_count, dtype=jnp.int32)
    ranks = jnp.arange(SEND_CAP, dtype=jnp.int32)
    select = (own_row[None, None, :] == targets[:, None, None]) & (
        send_rank[None, None, :] == ranks[None, :, None]
    )
    select = select.reshape(seq_count * SEND_CAP, block_count).astype(jnp.bfloat16)
    outgoing = jnp.dot(select, blocks_flat, preferred_element_type=jnp.float32).astype(jnp.bfloat16)
    outgoing_scales = jnp.dot(select, scales_flat, preferred_element_type=jnp.float32).astype(
        jnp.bfloat16
    )
    outgoing = outgoing.reshape(seq_count, SEND_CAP * 64 * col_width)
    outgoing_scales = outgoing_scales.reshape(seq_count, SEND_CAP * 64)
    incoming, incoming_scales = (
        lax.all_to_all(outgoing, "seq", split_axis=0, concat_axis=0, tiled=True),
        lax.all_to_all(outgoing_scales, "seq", split_axis=0, concat_axis=0, tiled=True),
    )
    owned_flags = (owner_grid == seq_index).astype(jnp.int32)
    recv_rank = jnp.sum(owned_flags[:, :, None] * earlier[None, :, :], axis=1)
    slot_hits = (owned_flags[:, None, :] == 1) & (recv_rank[:, None, :] == ranks[None, :, None])
    slot_of = jnp.sum(jnp.where(slot_hits, slot_grid[:, None, :] + 1, 0), axis=2) - 1
    slot_total = 2 * block_count
    placing = (
        slot_of.reshape(-1)[None, :] == jnp.arange(slot_total, dtype=jnp.int32)[:, None]
    ).astype(jnp.bfloat16)
    owner_cache = jnp.dot(
        placing,
        incoming.reshape(seq_count * SEND_CAP, 64 * col_width),
        preferred_element_type=jnp.float32,
    )
    owner_cache = owner_cache.astype(jnp.bfloat16).reshape(slot_total, 64, col_width)
    owner_scales = jnp.dot(
        placing,
        incoming_scales.reshape(seq_count * SEND_CAP, 64),
        preferred_element_type=jnp.float32,
    )
    return (owner_cache, owner_scales.astype(jnp.bfloat16))


def per_device(hidden, in_gain, kv_weight, kv_gain, block_owner, block_slot):
    seq_index = lax.axis_index("seq")
    tp_index = lax.axis_index("tp")
    gain_full = jnp.concatenate([kv_gain.astype(jnp.float32), jnp.ones((ROPE,), jnp.float32)])
    shard_rows = lax.all_gather(hidden, "tp", axis=0, tiled=True)
    normed = normalize(shard_rows, in_gain)
    row_total = shard_rows.shape[0]
    col_half = kv_weight.shape[1]
    projected = jnp.dot(
        normed,
        lax.all_gather(kv_weight, "seq", axis=0, tiled=True),
        preferred_element_type=jnp.float32,
    )
    col_index = tp_index * col_half + jnp.arange(col_half, dtype=jnp.int32)
    latent_part = jnp.where((col_index < LAT)[None, :], projected * projected, 0.0)
    power = lax.psum(jnp.sum(latent_part, axis=1), "tp")
    gain_cols = lax.dynamic_slice_in_dim(gain_full, tp_index * col_half, col_half, 0)
    positions = seq_index * row_total + jnp.arange(row_total, dtype=jnp.int32)
    shaped = shape_latent(projected, power, gain_cols, positions, col_index)
    token_peak = lax.pmax(jnp.max(jnp.abs(shaped), axis=1), "tp")
    token_scale = (token_peak + EPSILON).astype(jnp.bfloat16)
    quant = (shaped / token_scale.astype(jnp.float32)[:, None]).astype(jnp.bfloat16)
    return hand_off(quant, token_scale, block_owner, block_slot)


MESH = pl.DeviceIdType.MESH
X_COUNT = 2
Z_COUNT = 4
NT = (((1,), (1,)), ((), ()))
SCALE_ROWS = 16


def fused_kernel(
    owner_ref, slot_ref, hidden_ref, gain_ref, weight_ref, kv_gain_ref,
    cache_ref, scales_ref,
    weights, normed, select, placing, outgoing, incoming, stats_out, stats_in,
    hop_send, weight_recv, normed_sem, stats_sem, block_send, block_recv,
):
    group, seq, tp = lax.axis_index("group"), lax.axis_index("seq"), lax.axis_index("tp")
    n_seq = weights.shape[0]
    cols, depth = weights.shape[1:]
    rows = hidden_ref.shape[0]
    tokens = 2 * rows
    block_count = tokens // 64
    chunk = cols // 3
    z, x = seq // X_COUNT, seq % X_COUNT
    mine, middle, other = 2 * group, 1, 2 - 2 * group

    def at(z_to, x_to):
        return (group, z_to * X_COUNT + x_to, tp)

    above, below, beside = at(z + 1, x), at(z - 1, x), at(z, 1 - x)
    across, twin = (1 - group, seq, tp), (group, seq, 1 - tp)

    barrier = pltpu.get_barrier_semaphore()
    for step in range(1, n_seq):
        pl.semaphore_signal(
            barrier, inc=1, device_id=(group, (seq + step) % n_seq, tp), device_id_type=MESH
        )
    for peer in (across, twin):
        pl.semaphore_signal(barrier, inc=1, device_id=peer, device_id_type=MESH)

    row_id = lax.broadcasted_iota(jnp.int32, (cols, cols), 0)
    col_id = lax.broadcasted_iota(jnp.int32, (cols, cols), 1)
    eye = jnp.where(row_id == col_id, 1.0, 0.0).astype(jnp.bfloat16)
    weights[seq] = lax.dot_general(
        eye, weight_ref[...], NT, preferred_element_type=jnp.float32
    ).astype(jnp.bfloat16)
    pl.semaphore_wait(barrier, n_seq + 1)

    def piece(shard, part, direction, peer):
        where = weights.at[shard, pl.ds(pl.multiple_of(part * chunk, chunk), chunk), :]
        return pltpu.make_async_remote_copy(
            src_ref=where,
            dst_ref=where,
            send_sem=hop_send.at[shard, part, direction],
            recv_sem=weight_recv.at[shard, part],
            device_id=peer,
            device_id_type=MESH,
        )

    def when_inside(z_at, do):
        pl.when((z_at >= 0) & (z_at < Z_COUNT))(do)

    own = seq
    for part in (mine, middle):
        when_inside(z + 1, lambda: piece(own, part, 0, above).start())
        when_inside(z - 1, lambda: piece(own, part, 1, below).start())
        piece(own, part, 2, beside).start()

    first = pl.multiple_of(tp * rows, rows)

    def norm_tile(index, carry):
        tile = hidden_ref[pl.ds(pl.multiple_of(index * 16, 16), 16), :].astype(jnp.float32)
        power = jnp.mean(tile * tile, axis=1, keepdims=True)
        out = tile * lax.rsqrt(power + EPSILON) * gain_ref[...].astype(jnp.float32)
        normed[pl.ds(pl.multiple_of(first + index * 16, 16), 16), :] = out.astype(jnp.bfloat16)
        return carry

    lax.fori_loop(0, rows // 16, norm_tile, 0)
    half = normed.at[pl.ds(first, rows), :]
    normed_copy = pltpu.make_async_remote_copy(
        src_ref=half, dst_ref=half, send_sem=normed_sem.at[0], recv_sem=normed_sem.at[1],
        device_id=twin, device_id_type=MESH,
    )
    normed_copy.start()

    def rank_of(base, block):
        same = [
            jnp.where(owner_ref[base + earlier] == owner_ref[base + block], 1, 0)
            for earlier in range(block)
        ]
        return sum(same, jnp.int32(0))

    lane_id = lax.broadcasted_iota(jnp.int32, (64, n_seq * 128), 1)
    line_id = lax.broadcasted_iota(jnp.int32, (64, n_seq * 128), 0)
    for block in range(block_count):
        place = owner_ref[seq * block_count + block] * 128 + rank_of(seq * block_count, block) * 64
        select[pl.ds(block * 64, 64), :] = jnp.where(lane_id - line_id == place, 1.0, 0.0).astype(
            jnp.bfloat16
        )

    slot_total = cache_ref.shape[0] // 64
    lane_in = lax.broadcasted_iota(jnp.int32, (slot_total * 64, 128), 1)
    line_in = lax.broadcasted_iota(jnp.int32, (slot_total * 64, 128), 0)

    def slots_from(source):
        found = [jnp.int32(-1), jnp.int32(-1)]
        for block in range(block_count):
            entry = source * block_count + block
            rank = rank_of(source * block_count, block)
            for place in range(SEND_CAP):
                hit = (owner_ref[entry] == seq) & (rank == place)
                found[place] = jnp.where(hit, slot_ref[entry], found[place])
        return found

    slots = [slots_from(source) for source in range(n_seq)]
    for source in range(n_seq):
        low, high = slots[source]
        target = jnp.where(lane_in < 64, low * 64, high * 64) + lane_in % 64
        placing[:, source * 128 : (source + 1) * 128] = jnp.where(
            line_in == target, 1.0, 0.0
        ).astype(jnp.bfloat16)

    rope_half = ROPE // 2
    positions = lax.broadcasted_iota(jnp.int32, (rope_half, tokens), 1) + seq * tokens
    positions = positions.astype(jnp.float32)
    pair = lax.broadcasted_iota(jnp.int32, (rope_half, 1), 0)
    periods = jnp.zeros((rope_half, 1), jnp.float32)
    for index, period in enumerate(rope_periods(ROPE)):
        periods = jnp.where(pair == index, float(period), periods)
    turns = jnp.floor((positions + 0.5) / periods)
    phase = (positions - turns * periods) * (2.0 * math.pi) / periods
    cosine, sine = jnp.cos(phase), jnp.sin(phase)

    column = lax.broadcasted_iota(jnp.int32, (cols, LAT), 0) + tp * cols
    gain_lane = lax.broadcasted_iota(jnp.int32, (cols, LAT), 1)
    gain_col = jnp.sum(
        jnp.where(column == gain_lane, kv_gain_ref[...].astype(jnp.float32), 0.0),
        axis=1, keepdims=True,
    )

    def relay(z_from, x_from, onward):
        def do():
            shard = z_from * X_COUNT + x_from
            for part in (mine, middle):
                piece(shard, part, 2, beside).wait_recv()
                onward(shard, part)
                if part is mine:
                    piece(shard, part, 3, across).start()
        when_inside(z_from, do)

    def upward(shard, part):
        when_inside(z + 1, lambda: piece(shard, part, 0, above).start())
        piece(shard, part, 2, beside).start()

    def downward(shard, part):
        when_inside(z - 1, lambda: piece(shard, part, 1, below).start())
        piece(shard, part, 2, beside).start()

    def stop(shard, part):
        pass

    relay(z, 1 - x, stop)
    for distance in range(1, Z_COUNT):
        relay(z - distance, x, upward)
        relay(z + distance, x, downward)
        relay(z - distance, 1 - x, stop)
        relay(z + distance, 1 - x, stop)

    normed_copy.wait()
    total = jnp.zeros((cols, tokens), jnp.float32)
    for z_at in (z, z + 1 - 2 * (z % 2), (z + 2) % Z_COUNT, Z_COUNT - 1 - z):
        for x_at in (x, 1 - x):
            shard = z_at * X_COUNT + x_at
            if not (z_at is z and x_at is x):
                piece(shard, other, 3, across).wait_recv()
            features = pl.ds(pl.multiple_of(shard * depth, 128), depth)
            total = total + lax.dot_general(
                weights[shard], normed[:, features], NT, preferred_element_type=jnp.float32
            )

    latent = (lax.broadcasted_iota(jnp.int32, (cols, 1), 0) + tp * cols) < LAT
    gained = total * gain_col
    power = jnp.sum(jnp.where(latent, total * total, 0.0), axis=0, keepdims=True)
    latent_peak = jnp.max(jnp.where(latent, jnp.abs(gained), 0.0), axis=0, keepdims=True)
    lower = total[cols - ROPE : cols - rope_half, :]
    upper = total[cols - rope_half :, :]
    turned = jnp.concatenate(
        [lower * cosine - upper * sine, upper * cosine + lower * sine], axis=0
    )
    rope_peak = jnp.max(jnp.abs(turned), axis=0, keepdims=True)
    rope_peak = jnp.where(tp == 1, rope_peak, 0.0)
    stats_out[0:1, :] = power
    stats_out[1:2, :] = latent_peak
    stats_out[2:3, :] = rope_peak
    stats_out[3:8, :] = jnp.zeros((5, tokens), jnp.float32)
    stats_copy = pltpu.make_async_remote_copy(
        src_ref=stats_out, dst_ref=stats_in, send_sem=stats_sem.at[0], recv_sem=stats_sem.at[1],
        device_id=twin, device_id_type=MESH,
    )
    stats_copy.start()
    stats_copy.wait()
    inverse = lax.rsqrt((power + stats_in[0:1, :]) / LAT + EPSILON)
    peak = jnp.maximum(
        jnp.maximum(latent_peak, stats_in[1:2, :]) * inverse,
        jnp.maximum(rope_peak, stats_in[2:3, :]),
    )
    scale = (peak + EPSILON).astype(jnp.bfloat16)
    wide_scale = scale.astype(jnp.float32)
    shaped = jnp.where(
        latent,
        gained * inverse,
        jnp.concatenate([jnp.zeros((cols - ROPE, tokens), jnp.float32), turned], axis=0),
    )
    quant = (shaped / wide_scale).astype(jnp.bfloat16)
    with_scale = jnp.concatenate(
        [quant, jnp.broadcast_to(wide_scale, (SCALE_ROWS, tokens)).astype(jnp.bfloat16)], axis=0
    )

    for target in range(n_seq):
        outgoing[target] = jnp.dot(
            with_scale, select[:, target * 128 : (target + 1) * 128],
            preferred_element_type=jnp.float32,
        ).astype(jnp.bfloat16)

    def block_copy(source, target):
        return pltpu.make_async_remote_copy(
            src_ref=outgoing.at[target], dst_ref=incoming.at[source],
            send_sem=block_send.at[target], recv_sem=block_recv.at[source],
            device_id=(group, target, tp), device_id_type=MESH,
        )

    for step in range(1, n_seq):
        block_copy(seq, (seq + step) % n_seq).start()
    incoming[seq] = outgoing[seq]
    for step in range(1, n_seq):
        source = (seq + step) % n_seq
        block_copy(source, source).wait_recv()
    arrived = jnp.concatenate([incoming[source, :cols, :] for source in range(n_seq)], axis=1)
    cache_ref[...] = lax.dot_general(
        placing[...], arrived, NT, preferred_element_type=jnp.float32
    ).astype(jnp.bfloat16)
    slot_id = lax.broadcasted_iota(jnp.int32, (slot_total, 128), 0)
    lane = lax.broadcasted_iota(jnp.int32, (slot_total, 128), 1)
    placed = jnp.zeros((slot_total, 128), jnp.float32)
    for source in range(n_seq):
        low, high = slots[source]
        hit = slot_id == jnp.where(lane < 64, low, high)
        values = incoming[source, cols : cols + SCALE_ROWS, :].astype(jnp.float32)
        placed = placed + jnp.where(hit, values[0:slot_total, :], 0.0)
    scales_ref[...] = (placed[:, :64] + placed[:, 64:]).astype(jnp.bfloat16)

    for step in range(1, n_seq):
        block_copy(seq, (seq + step) % n_seq).wait_send()
    for part in (mine, middle):
        when_inside(z + 1, lambda: piece(own, part, 0, above).wait_send())
        when_inside(z - 1, lambda: piece(own, part, 1, below).wait_send())
        piece(own, part, 2, beside).wait_send()

    def sent(z_from, x_from, direction, z_to, peer):
        def do():
            shard = z_from * X_COUNT + x_from
            for part in (mine, middle):
                if direction is not None:
                    when_inside(z_to, lambda: piece(shard, part, direction, peer).wait_send())
                    piece(shard, part, 2, beside).wait_send()
            piece(shard, mine, 3, across).wait_send()
        when_inside(z_from, do)

    sent(z, 1 - x, None, None, None)
    for distance in range(1, Z_COUNT):
        sent(z - distance, x, 0, z + 1, above)
        sent(z + distance, x, 1, z - 1, below)
        sent(z - distance, 1 - x, None, None, None)
        sent(z + distance, 1 - x, None, None, None)


def fused(hidden, in_gain, kv_weight, kv_gain, block_owner, block_slot):
    rows, width = hidden.shape
    depth, cols = kv_weight.shape
    n_seq = lax.axis_size("seq")
    tokens = 2 * rows
    slot_total = 2 * (tokens // 64)
    padded = cols + SCALE_ROWS
    vmem = pl.BlockSpec(memory_space=pltpu.VMEM)
    smem = pl.BlockSpec(memory_space=pltpu.SMEM)
    cache, scales = pl.pallas_call(
        fused_kernel,
        out_shape=(
            jax.ShapeDtypeStruct((slot_total * 64, cols), jnp.bfloat16),
            jax.ShapeDtypeStruct((slot_total, 64), jnp.bfloat16),
        ),
        in_specs=[smem, smem, vmem, vmem, vmem, vmem],
        out_specs=(vmem, vmem),
        scratch_shapes=[
            pltpu.VMEM((n_seq, cols, depth), jnp.bfloat16),
            pltpu.VMEM((tokens, width), jnp.bfloat16),
            pltpu.VMEM((tokens, n_seq * 128), jnp.bfloat16),
            pltpu.VMEM((slot_total * 64, n_seq * 128), jnp.bfloat16),
            pltpu.VMEM((n_seq, padded, 128), jnp.bfloat16),
            pltpu.VMEM((n_seq, padded, 128), jnp.bfloat16),
            pltpu.VMEM((8, tokens), jnp.float32),
            pltpu.VMEM((8, tokens), jnp.float32),
            pltpu.SemaphoreType.DMA((n_seq, 3, 4)),
            pltpu.SemaphoreType.DMA((n_seq, 3)),
            pltpu.SemaphoreType.DMA((2,)),
            pltpu.SemaphoreType.DMA((2,)),
            pltpu.SemaphoreType.DMA((n_seq,)),
            pltpu.SemaphoreType.DMA((n_seq,)),
        ],
        compiler_params=pltpu.CompilerParams(
            collective_id=0, has_side_effects=True, vmem_limit_bytes=48 * 1024 * 1024
        ),
    )(
        block_owner, block_slot, hidden, in_gain.reshape(1, width), kv_weight,
        kv_gain.reshape(1, LAT),
    )
    return (cache.reshape(slot_total, 64, cols), scales)


def solution(mesh):
    fits = (
        mesh.shape["seq"] == X_COUNT * Z_COUNT
        and mesh.shape["group"] == 2
        and mesh.shape["tp"] == 2
    )
    return jax.shard_map(
        fused if fits else per_device,
        mesh=mesh,
        in_specs=(P(("group", "seq", "tp"), None), P(), P("seq", "tp"), P(), P(), P()),
        out_specs=(P(("group", "seq"), None, "tp"), P(("group", "seq"), None)),
        check_vma=False,
    )
```

```python
import functools
import math

import jax
import jax.numpy as jnp
import numpy as np
from jax import lax
from jax.experimental import pallas as pl
from jax.experimental.pallas import tpu as pltpu
from jax.sharding import PartitionSpec as P

LAT = 512
ROPE = 64
SEND_CAP = 2


EPSILON = 1e-06


def rope_periods(rope_width):
    return np.floor(
        2.0 * np.pi * 10000.0 ** (np.arange(rope_width // 2) * 2.0 / rope_width) + 0.5
    ).astype(np.int32)


def normalize(values, in_gain):
    wide = values.astype(jnp.float32)
    power = jnp.mean(wide * wide, axis=1, keepdims=True)
    return (wide * lax.rsqrt(power + EPSILON) * in_gain.astype(jnp.float32)).astype(jnp.bfloat16)


def shape_latent(projected, power, gain_cols, positions, col_index):
    scaled = projected * lax.rsqrt(power / LAT + EPSILON)[:, None] * gain_cols[None, :]
    periods = jnp.asarray(rope_periods(ROPE))
    phase = (
        (positions[:, None] % periods[None, :]).astype(jnp.float32)
        * (2.0 * math.pi)
        / periods.astype(jnp.float32)
    )
    cosine = jnp.cos(phase)
    sine = jnp.sin(phase)
    col_total = projected.shape[1]
    rope_tail = projected[:, col_total - ROPE :]
    lower_half = rope_tail[:, : ROPE // 2]
    upper_half = rope_tail[:, ROPE // 2 :]
    rotated = jnp.concatenate(
        [lower_half * cosine - upper_half * sine, upper_half * cosine + lower_half * sine], axis=1
    )
    rotated_full = jnp.concatenate([projected[:, : col_total - ROPE], rotated], axis=1)
    return jnp.where((col_index >= LAT)[None, :], rotated_full, scaled)


def hand_off(quant, token_scale, block_owner, block_slot):
    seq_count = lax.axis_size("seq")
    seq_index = lax.axis_index("seq")
    block_count = quant.shape[0] // 64
    col_width = quant.shape[1]
    blocks_flat = quant.reshape(block_count, 64 * col_width)
    scales_flat = token_scale.reshape(block_count, 64)
    owner_grid = block_owner.reshape(seq_count, block_count)
    slot_grid = block_slot.reshape(seq_count, block_count)
    earlier = (jnp.arange(block_count)[:, None] < jnp.arange(block_count)[None, :]).astype(
        jnp.int32
    )
    own_row = lax.dynamic_slice_in_dim(owner_grid, seq_index, 1, 0)[0]
    same_owner = (own_row[:, None] == own_row[None, :]).astype(jnp.int32)
    send_rank = jnp.sum(same_owner * earlier, axis=0)
    targets = jnp.arange(seq_count, dtype=jnp.int32)
    ranks = jnp.arange(SEND_CAP, dtype=jnp.int32)
    select = (own_row[None, None, :] == targets[:, None, None]) & (
        send_rank[None, None, :] == ranks[None, :, None]
    )
    select = select.reshape(seq_count * SEND_CAP, block_count).astype(jnp.bfloat16)
    outgoing = jnp.dot(select, blocks_flat, preferred_element_type=jnp.float32).astype(jnp.bfloat16)
    outgoing_scales = jnp.dot(select, scales_flat, preferred_element_type=jnp.float32).astype(
        jnp.bfloat16
    )
    outgoing = outgoing.reshape(seq_count, SEND_CAP * 64 * col_width)
    outgoing_scales = outgoing_scales.reshape(seq_count, SEND_CAP * 64)
    incoming, incoming_scales = (
        lax.all_to_all(outgoing, "seq", split_axis=0, concat_axis=0, tiled=True),
        lax.all_to_all(outgoing_scales, "seq", split_axis=0, concat_axis=0, tiled=True),
    )
    owned_flags = (owner_grid == seq_index).astype(jnp.int32)
    recv_rank = jnp.sum(owned_flags[:, :, None] * earlier[None, :, :], axis=1)
    slot_hits = (owned_flags[:, None, :] == 1) & (recv_rank[:, None, :] == ranks[None, :, None])
    slot_of = jnp.sum(jnp.where(slot_hits, slot_grid[:, None, :] + 1, 0), axis=2) - 1
    slot_total = 2 * block_count
    placing = (
        slot_of.reshape(-1)[None, :] == jnp.arange(slot_total, dtype=jnp.int32)[:, None]
    ).astype(jnp.bfloat16)
    owner_cache = jnp.dot(
        placing,
        incoming.reshape(seq_count * SEND_CAP, 64 * col_width),
        preferred_element_type=jnp.float32,
    )
    owner_cache = owner_cache.astype(jnp.bfloat16).reshape(slot_total, 64, col_width)
    owner_scales = jnp.dot(
        placing,
        incoming_scales.reshape(seq_count * SEND_CAP, 64),
        preferred_element_type=jnp.float32,
    )
    return (owner_cache, owner_scales.astype(jnp.bfloat16))


def per_device(hidden, in_gain, kv_weight, kv_gain, block_owner, block_slot):
    seq_index = lax.axis_index("seq")
    tp_index = lax.axis_index("tp")
    gain_full = jnp.concatenate([kv_gain.astype(jnp.float32), jnp.ones((ROPE,), jnp.float32)])
    shard_rows = lax.all_gather(hidden, "tp", axis=0, tiled=True)
    normed = normalize(shard_rows, in_gain)
    row_total = shard_rows.shape[0]
    col_half = kv_weight.shape[1]
    projected = jnp.dot(
        normed,
        lax.all_gather(kv_weight, "seq", axis=0, tiled=True),
        preferred_element_type=jnp.float32,
    )
    col_index = tp_index * col_half + jnp.arange(col_half, dtype=jnp.int32)
    latent_part = jnp.where((col_index < LAT)[None, :], projected * projected, 0.0)
    power = lax.psum(jnp.sum(latent_part, axis=1), "tp")
    gain_cols = lax.dynamic_slice_in_dim(gain_full, tp_index * col_half, col_half, 0)
    positions = seq_index * row_total + jnp.arange(row_total, dtype=jnp.int32)
    shaped = shape_latent(projected, power, gain_cols, positions, col_index)
    token_peak = lax.pmax(jnp.max(jnp.abs(shaped), axis=1), "tp")
    token_scale = (token_peak + EPSILON).astype(jnp.bfloat16)
    quant = (shaped / token_scale.astype(jnp.float32)[:, None]).astype(jnp.bfloat16)
    return hand_off(quant, token_scale, block_owner, block_slot)


MESH = pl.DeviceIdType.MESH
X_COUNT = 2
Z_COUNT = 4
NT = (((1,), (1,)), ((), ()))
SCALE_ROWS = 16


def fused_kernel(
    owner_hbm, slot_hbm, hidden_hbm, gain_hbm, weight_hbm, kv_gain_hbm,
    cache_ref, scales_ref,
    owner_ref, slot_ref, hidden_ref, gain_ref, kv_gain_ref, gain_row, load_sem,
    weights, normed, select, placing, outgoing, incoming, stats_out, stats_in,
    hop_send, weight_recv, normed_sem, stats_sem, block_send, block_recv,
):
    group, seq, tp = lax.axis_index("group"), lax.axis_index("seq"), lax.axis_index("tp")
    n_seq = weights.shape[0]
    cols, depth = weights.shape[1:]
    rows = hidden_ref.shape[0]
    tokens = 2 * rows
    block_count = tokens // 64
    chunk = cols // 3
    z, x = seq // X_COUNT, seq % X_COUNT
    mine, middle, other = 2 * group, 1, 2 - 2 * group

    def at(z_to, x_to):
        return (group, z_to * X_COUNT + x_to, tp)

    above, below, beside = at(z + 1, x), at(z - 1, x), at(z, 1 - x)
    across, twin = (1 - group, seq, tp), (group, seq, 1 - tp)

    loads = [
        pltpu.make_async_copy(source, target, load_sem.at[index])
        for index, (source, target) in enumerate((
            (hidden_hbm, hidden_ref), (gain_hbm, gain_ref), (weight_hbm, weights.at[seq]),
            (kv_gain_hbm, kv_gain_ref), (owner_hbm, owner_ref), (slot_hbm, slot_ref),
        ))
    ]
    for load in loads:
        load.start()

    barrier = pltpu.get_barrier_semaphore()
    for step in range(1, n_seq):
        pl.semaphore_signal(
            barrier, inc=1, device_id=(group, (seq + step) % n_seq, tp), device_id_type=MESH
        )
    for peer in (across, twin):
        pl.semaphore_signal(barrier, inc=1, device_id=peer, device_id_type=MESH)

    pl.semaphore_wait(barrier, n_seq + 1)

    def piece(shard, part, direction, peer, source=None):
        lines = pl.ds(pl.multiple_of(part * chunk, chunk), chunk)
        where = weights.at[shard, lines, :]
        return pltpu.make_async_remote_copy(
            src_ref=where if source is None else source.at[lines, :],
            dst_ref=where,
            send_sem=hop_send.at[shard, part, direction],
            recv_sem=weight_recv.at[shard, part],
            device_id=peer,
            device_id_type=MESH,
        )

    def when_inside(z_at, do):
        pl.when((z_at >= 0) & (z_at < Z_COUNT))(do)

    own = seq
    for part in (mine, middle):
        when_inside(z + 1, lambda: piece(own, part, 0, above, weight_hbm).start())
        when_inside(z - 1, lambda: piece(own, part, 1, below, weight_hbm).start())
        piece(own, part, 2, beside, weight_hbm).start()

    for load in loads:
        load.wait()
    for line in range(gain_ref.shape[0]):
        gain_row[0:1, line * 128 : (line + 1) * 128] = gain_ref[line : line + 1, :].astype(
            jnp.float32
        )
    first = pl.multiple_of(tp * rows, rows)

    def norm_tile(index, carry):
        tile = hidden_ref[pl.ds(pl.multiple_of(index * 16, 16), 16), :].astype(jnp.float32)
        power = jnp.mean(tile * tile, axis=1, keepdims=True)
        out = tile * lax.rsqrt(power + EPSILON) * gain_row[0:1, :]
        normed[pl.ds(pl.multiple_of(first + index * 16, 16), 16), :] = out.astype(jnp.bfloat16)
        return carry

    lax.fori_loop(0, rows // 16, norm_tile, 0)
    half = normed.at[pl.ds(first, rows), :]
    normed_copy = pltpu.make_async_remote_copy(
        src_ref=half, dst_ref=half, send_sem=normed_sem.at[0], recv_sem=normed_sem.at[1],
        device_id=twin, device_id_type=MESH,
    )
    normed_copy.start()

    def arrive(z_from, x_from, part, step=0):
        def do():
            shard = z_from * X_COUNT + x_from
            piece(shard, part, 2, beside).wait_recv()
            if part is mine:
                piece(shard, part, 3, across).start()
            if step == 1:
                when_inside(z + 1, lambda: piece(shard, part, 0, above).start())
            if step == -1:
                when_inside(z - 1, lambda: piece(shard, part, 1, below).start())
            if step != 0:
                piece(shard, part, 2, beside).start()
        when_inside(z_from, do)

    def arrive_column(distance, part):
        arrive(z - distance, x, part, 1)
        arrive(z + distance, x, part, -1)

    def arrive_beside(distance, part):
        arrive(z - distance, 1 - x, part)
        if distance:
            arrive(z + distance, 1 - x, part)

    arrive_column(1, mine)
    arrive_beside(0, mine)

    def rank_of(base, block):
        same = [
            jnp.where(owner_ref[base + earlier] == owner_ref[base + block], 1, 0)
            for earlier in range(block)
        ]
        return sum(same, jnp.int32(0))

    lane_id = lax.broadcasted_iota(jnp.int32, (64, n_seq * 128), 1)
    line_id = lax.broadcasted_iota(jnp.int32, (64, n_seq * 128), 0)
    for block in range(block_count):
        place = owner_ref[seq * block_count + block] * 128 + rank_of(seq * block_count, block) * 64
        select[pl.ds(block * 64, 64), :] = jnp.where(lane_id - line_id == place, 1.0, 0.0).astype(
            jnp.bfloat16
        )

    arrive_column(2, mine)
    arrive_beside(1, mine)

    slot_total = cache_ref.shape[0] // 64
    lane_in = lax.broadcasted_iota(jnp.int32, (slot_total * 64, 128), 1)
    line_in = lax.broadcasted_iota(jnp.int32, (slot_total * 64, 128), 0)

    def slots_from(source):
        found = [jnp.int32(-1), jnp.int32(-1)]
        for block in range(block_count):
            entry = source * block_count + block
            rank = rank_of(source * block_count, block)
            for place in range(SEND_CAP):
                hit = (owner_ref[entry] == seq) & (rank == place)
                found[place] = jnp.where(hit, slot_ref[entry], found[place])
        return found

    slots = [slots_from(source) for source in range(n_seq)]
    for source in range(n_seq):
        low, high = slots[source]
        target = jnp.where(lane_in < 64, low * 64, high * 64) + lane_in % 64
        placing[:, source * 128 : (source + 1) * 128] = jnp.where(
            line_in == target, 1.0, 0.0
        ).astype(jnp.bfloat16)

    arrive_column(3, mine)
    arrive_column(1, middle)

    rope_half = ROPE // 2
    positions = lax.broadcasted_iota(jnp.int32, (rope_half, tokens), 1) + seq * tokens
    positions = positions.astype(jnp.float32)
    pair = lax.broadcasted_iota(jnp.int32, (rope_half, 1), 0)
    periods = jnp.zeros((rope_half, 1), jnp.float32)
    for index, period in enumerate(rope_periods(ROPE)):
        periods = jnp.where(pair == index, float(period), periods)
    turns = jnp.floor((positions + 0.5) / periods)
    phase = (positions - turns * periods) * (2.0 * math.pi) / periods
    cosine, sine = jnp.cos(phase), jnp.sin(phase)

    column = lax.broadcasted_iota(jnp.int32, (cols, LAT), 0) + tp * cols
    gain_lane = lax.broadcasted_iota(jnp.int32, (cols, LAT), 1)
    gain_all = jnp.concatenate(
        [kv_gain_ref[line : line + 1, :].astype(jnp.float32) for line in range(LAT // 128)], axis=1
    )
    gain_col = jnp.sum(jnp.where(column == gain_lane, gain_all, 0.0), axis=1, keepdims=True)

    arrive_beside(2, mine)
    arrive_column(2, middle)
    arrive_beside(3, mine)
    arrive_column(3, middle)

    normed_copy.wait()
    total = jnp.zeros((cols, tokens), jnp.float32)
    z_order = (z, z + 1 - 2 * (z % 2), (z + 2) % Z_COUNT, Z_COUNT - 1 - z)
    for x_at in (x, 1 - x):
        for z_at in z_order:
            shard = z_at * X_COUNT + x_at
            if x_at is not x:
                piece(shard, middle, 2, beside).wait_recv()
            if not (z_at is z and x_at is x):
                piece(shard, other, 3, across).wait_recv()
            features = pl.ds(pl.multiple_of(shard * depth, 128), depth)
            total = total + lax.dot_general(
                weights[shard], normed[:, features], NT, preferred_element_type=jnp.float32
            )

    latent = (lax.broadcasted_iota(jnp.int32, (cols, 1), 0) + tp * cols) < LAT
    gained = total * gain_col
    power = jnp.sum(jnp.where(latent, total * total, 0.0), axis=0, keepdims=True)
    latent_peak = jnp.max(jnp.where(latent, jnp.abs(gained), 0.0), axis=0, keepdims=True)
    lower = total[cols - ROPE : cols - rope_half, :]
    upper = total[cols - rope_half :, :]
    turned = jnp.concatenate(
        [lower * cosine - upper * sine, upper * cosine + lower * sine], axis=0
    )
    rope_peak = jnp.max(jnp.abs(turned), axis=0, keepdims=True)
    rope_peak = jnp.where(tp == 1, rope_peak, 0.0)
    stats_out[0:1, :] = power
    stats_out[1:2, :] = latent_peak
    stats_out[2:3, :] = rope_peak
    stats_out[3:8, :] = jnp.zeros((5, tokens), jnp.float32)
    stats_copy = pltpu.make_async_remote_copy(
        src_ref=stats_out, dst_ref=stats_in, send_sem=stats_sem.at[0], recv_sem=stats_sem.at[1],
        device_id=twin, device_id_type=MESH,
    )
    stats_copy.start()
    stats_copy.wait()
    inverse = lax.rsqrt((power + stats_in[0:1, :]) / LAT + EPSILON)
    peak = jnp.maximum(
        jnp.maximum(latent_peak, stats_in[1:2, :]) * inverse,
        jnp.maximum(rope_peak, stats_in[2:3, :]),
    )
    scale = (peak + EPSILON).astype(jnp.bfloat16)
    wide_scale = scale.astype(jnp.float32)
    shaped = jnp.where(
        latent,
        gained * inverse,
        jnp.concatenate([jnp.zeros((cols - ROPE, tokens), jnp.float32), turned], axis=0),
    )
    quant = (shaped / wide_scale).astype(jnp.bfloat16)
    with_scale = jnp.concatenate(
        [quant, jnp.broadcast_to(wide_scale, (SCALE_ROWS, tokens)).astype(jnp.bfloat16)], axis=0
    )

    for target in range(n_seq):
        outgoing[target] = jnp.dot(
            with_scale, select[:, target * 128 : (target + 1) * 128],
            preferred_element_type=jnp.float32,
        ).astype(jnp.bfloat16)

    def block_copy(source, target):
        return pltpu.make_async_remote_copy(
            src_ref=outgoing.at[target], dst_ref=incoming.at[source],
            send_sem=block_send.at[target], recv_sem=block_recv.at[source],
            device_id=(group, target, tp), device_id_type=MESH,
        )

    for step in range(1, n_seq):
        block_copy(seq, (seq + step) % n_seq).start()
    incoming[seq] = outgoing[seq]
    for step in range(1, n_seq):
        source = (seq + step) % n_seq
        block_copy(source, source).wait_recv()
    arrived = jnp.concatenate([incoming[source, :cols, :] for source in range(n_seq)], axis=1)
    cache_ref[...] = lax.dot_general(
        placing[...], arrived, NT, preferred_element_type=jnp.float32
    ).astype(jnp.bfloat16)
    slot_id = lax.broadcasted_iota(jnp.int32, (slot_total, 128), 0)
    lane = lax.broadcasted_iota(jnp.int32, (slot_total, 128), 1)
    placed = jnp.zeros((slot_total, 128), jnp.float32)
    for source in range(n_seq):
        low, high = slots[source]
        hit = slot_id == jnp.where(lane < 64, low, high)
        values = incoming[source, cols : cols + SCALE_ROWS, :].astype(jnp.float32)
        placed = placed + jnp.where(hit, values[0:slot_total, :], 0.0)
    scales_ref[...] = (placed[:, :64] + placed[:, 64:]).astype(jnp.bfloat16)

    for step in range(1, n_seq):
        block_copy(seq, (seq + step) % n_seq).wait_send()
    for part in (mine, middle):
        when_inside(z + 1, lambda: piece(own, part, 0, above, weight_hbm).wait_send())
        when_inside(z - 1, lambda: piece(own, part, 1, below, weight_hbm).wait_send())
        piece(own, part, 2, beside, weight_hbm).wait_send()

    def sent(z_from, x_from, direction, z_to, peer):
        def do():
            shard = z_from * X_COUNT + x_from
            for part in (mine, middle):
                if direction is not None:
                    when_inside(z_to, lambda: piece(shard, part, direction, peer).wait_send())
                    piece(shard, part, 2, beside).wait_send()
            piece(shard, mine, 3, across).wait_send()
        when_inside(z_from, do)

    sent(z, 1 - x, None, None, None)
    for distance in range(1, Z_COUNT):
        sent(z - distance, x, 0, z + 1, above)
        sent(z + distance, x, 1, z - 1, below)
        sent(z - distance, 1 - x, None, None, None)
        sent(z + distance, 1 - x, None, None, None)


def fused(hidden, in_gain, kv_weight, kv_gain, block_owner, block_slot):
    rows, width = hidden.shape
    depth, cols = kv_weight.shape
    n_seq = lax.axis_size("seq")
    tokens = 2 * rows
    slot_total = 2 * (tokens // 64)
    padded = cols + SCALE_ROWS
    vmem = pl.BlockSpec(memory_space=pltpu.VMEM)
    hbm = pl.BlockSpec(memory_space=pltpu.HBM)
    cache, scales = pl.pallas_call(
        fused_kernel,
        out_shape=(
            jax.ShapeDtypeStruct((slot_total * 64, cols), jnp.bfloat16),
            jax.ShapeDtypeStruct((slot_total, 64), jnp.bfloat16),
        ),
        in_specs=[hbm] * 6,
        out_specs=(vmem, vmem),
        scratch_shapes=[
            pltpu.SMEM(block_owner.shape, jnp.int32),
            pltpu.SMEM(block_slot.shape, jnp.int32),
            pltpu.VMEM((rows, width), jnp.bfloat16),
            pltpu.VMEM((width // 128, 128), jnp.bfloat16),
            pltpu.VMEM((LAT // 128, 128), jnp.bfloat16),
            pltpu.VMEM((8, width), jnp.float32),
            pltpu.SemaphoreType.DMA((6,)),
            pltpu.VMEM((n_seq, cols, depth), jnp.bfloat16),
            pltpu.VMEM((tokens, width), jnp.bfloat16),
            pltpu.VMEM((tokens, n_seq * 128), jnp.bfloat16),
            pltpu.VMEM((slot_total * 64, n_seq * 128), jnp.bfloat16),
            pltpu.VMEM((n_seq, padded, 128), jnp.bfloat16),
            pltpu.VMEM((n_seq, padded, 128), jnp.bfloat16),
            pltpu.VMEM((8, tokens), jnp.float32),
            pltpu.VMEM((8, tokens), jnp.float32),
            pltpu.SemaphoreType.DMA((n_seq, 3, 4)),
            pltpu.SemaphoreType.DMA((n_seq, 3)),
            pltpu.SemaphoreType.DMA((2,)),
            pltpu.SemaphoreType.DMA((2,)),
            pltpu.SemaphoreType.DMA((n_seq,)),
            pltpu.SemaphoreType.DMA((n_seq,)),
        ],
        compiler_params=pltpu.CompilerParams(
            collective_id=0, has_side_effects=True, vmem_limit_bytes=64 * 1024 * 1024 - 65536
        ),
    )(
        block_owner, block_slot, hidden, in_gain.reshape(width // 128, 128), kv_weight.T,
        kv_gain.reshape(LAT // 128, 128),
    )
    return (cache.reshape(slot_total, 64, cols), scales)


def solution(mesh):
    fits = (
        mesh.shape["seq"] == X_COUNT * Z_COUNT
        and mesh.shape["group"] == 2
        and mesh.shape["tp"] == 2
    )
    return jax.shard_map(
        fused if fits else per_device,
        mesh=mesh,
        in_specs=(P(("group", "seq", "tp"), None), P(), P("seq", "tp"), P(), P(), P()),
        out_specs=(P(("group", "seq"), None, "tp"), P(("group", "seq"), None)),
        check_vma=False,
    )
```

```python
import functools
import functools
import math

import jax
import jax.numpy as jnp
import numpy as np
from jax import lax
from jax.experimental import pallas as pl
from jax.experimental.pallas import tpu as pltpu
from jax.sharding import PartitionSpec as P

LAT = 512
ROPE = 64
SEND_CAP = 2


EPSILON = 1e-06


def rope_periods(rope_width):
    return np.floor(
        2.0 * np.pi * 10000.0 ** (np.arange(rope_width // 2) * 2.0 / rope_width) + 0.5
    ).astype(np.int32)


def normalize(values, in_gain):
    wide = values.astype(jnp.float32)
    power = jnp.mean(wide * wide, axis=1, keepdims=True)
    return (wide * lax.rsqrt(power + EPSILON) * in_gain.astype(jnp.float32)).astype(jnp.bfloat16)


def shape_latent(projected, power, gain_cols, positions, col_index):
    scaled = projected * lax.rsqrt(power / LAT + EPSILON)[:, None] * gain_cols[None, :]
    periods = jnp.asarray(rope_periods(ROPE))
    phase = (
        (positions[:, None] % periods[None, :]).astype(jnp.float32)
        * (2.0 * math.pi)
        / periods.astype(jnp.float32)
    )
    cosine = jnp.cos(phase)
    sine = jnp.sin(phase)
    col_total = projected.shape[1]
    rope_tail = projected[:, col_total - ROPE :]
    lower_half = rope_tail[:, : ROPE // 2]
    upper_half = rope_tail[:, ROPE // 2 :]
    rotated = jnp.concatenate(
        [lower_half * cosine - upper_half * sine, upper_half * cosine + lower_half * sine], axis=1
    )
    rotated_full = jnp.concatenate([projected[:, : col_total - ROPE], rotated], axis=1)
    return jnp.where((col_index >= LAT)[None, :], rotated_full, scaled)


def hand_off(quant, token_scale, block_owner, block_slot):
    seq_count = lax.axis_size("seq")
    seq_index = lax.axis_index("seq")
    block_count = quant.shape[0] // 64
    col_width = quant.shape[1]
    blocks_flat = quant.reshape(block_count, 64 * col_width)
    scales_flat = token_scale.reshape(block_count, 64)
    owner_grid = block_owner.reshape(seq_count, block_count)
    slot_grid = block_slot.reshape(seq_count, block_count)
    earlier = (jnp.arange(block_count)[:, None] < jnp.arange(block_count)[None, :]).astype(
        jnp.int32
    )
    own_row = lax.dynamic_slice_in_dim(owner_grid, seq_index, 1, 0)[0]
    same_owner = (own_row[:, None] == own_row[None, :]).astype(jnp.int32)
    send_rank = jnp.sum(same_owner * earlier, axis=0)
    targets = jnp.arange(seq_count, dtype=jnp.int32)
    ranks = jnp.arange(SEND_CAP, dtype=jnp.int32)
    select = (own_row[None, None, :] == targets[:, None, None]) & (
        send_rank[None, None, :] == ranks[None, :, None]
    )
    select = select.reshape(seq_count * SEND_CAP, block_count).astype(jnp.bfloat16)
    outgoing = jnp.dot(select, blocks_flat, preferred_element_type=jnp.float32).astype(jnp.bfloat16)
    outgoing_scales = jnp.dot(select, scales_flat, preferred_element_type=jnp.float32).astype(
        jnp.bfloat16
    )
    outgoing = outgoing.reshape(seq_count, SEND_CAP * 64 * col_width)
    outgoing_scales = outgoing_scales.reshape(seq_count, SEND_CAP * 64)
    incoming, incoming_scales = (
        lax.all_to_all(outgoing, "seq", split_axis=0, concat_axis=0, tiled=True),
        lax.all_to_all(outgoing_scales, "seq", split_axis=0, concat_axis=0, tiled=True),
    )
    owned_flags = (owner_grid == seq_index).astype(jnp.int32)
    recv_rank = jnp.sum(owned_flags[:, :, None] * earlier[None, :, :], axis=1)
    slot_hits = (owned_flags[:, None, :] == 1) & (recv_rank[:, None, :] == ranks[None, :, None])
    slot_of = jnp.sum(jnp.where(slot_hits, slot_grid[:, None, :] + 1, 0), axis=2) - 1
    slot_total = 2 * block_count
    placing = (
        slot_of.reshape(-1)[None, :] == jnp.arange(slot_total, dtype=jnp.int32)[:, None]
    ).astype(jnp.bfloat16)
    owner_cache = jnp.dot(
        placing,
        incoming.reshape(seq_count * SEND_CAP, 64 * col_width),
        preferred_element_type=jnp.float32,
    )
    owner_cache = owner_cache.astype(jnp.bfloat16).reshape(slot_total, 64, col_width)
    owner_scales = jnp.dot(
        placing,
        incoming_scales.reshape(seq_count * SEND_CAP, 64),
        preferred_element_type=jnp.float32,
    )
    return (owner_cache, owner_scales.astype(jnp.bfloat16))


def per_device(hidden, in_gain, kv_weight, kv_gain, block_owner, block_slot):
    seq_index = lax.axis_index("seq")
    tp_index = lax.axis_index("tp")
    gain_full = jnp.concatenate([kv_gain.astype(jnp.float32), jnp.ones((ROPE,), jnp.float32)])
    shard_rows = lax.all_gather(hidden, "tp", axis=0, tiled=True)
    normed = normalize(shard_rows, in_gain)
    row_total = shard_rows.shape[0]
    col_half = kv_weight.shape[1]
    projected = jnp.dot(
        normed,
        lax.all_gather(kv_weight, "seq", axis=0, tiled=True),
        preferred_element_type=jnp.float32,
    )
    col_index = tp_index * col_half + jnp.arange(col_half, dtype=jnp.int32)
    latent_part = jnp.where((col_index < LAT)[None, :], projected * projected, 0.0)
    power = lax.psum(jnp.sum(latent_part, axis=1), "tp")
    gain_cols = lax.dynamic_slice_in_dim(gain_full, tp_index * col_half, col_half, 0)
    positions = seq_index * row_total + jnp.arange(row_total, dtype=jnp.int32)
    shaped = shape_latent(projected, power, gain_cols, positions, col_index)
    token_peak = lax.pmax(jnp.max(jnp.abs(shaped), axis=1), "tp")
    token_scale = (token_peak + EPSILON).astype(jnp.bfloat16)
    quant = (shaped / token_scale.astype(jnp.float32)[:, None]).astype(jnp.bfloat16)
    return hand_off(quant, token_scale, block_owner, block_slot)


MESH = pl.DeviceIdType.MESH
X_COUNT = 2
Z_COUNT = 4
NT = (((1,), (1,)), ((), ()))
SCALE_ROWS = 16


def fused_kernel(
    owner_hbm, slot_hbm, hidden_hbm, gain_hbm, weight_hbm, kv_gain_hbm,
    cache_ref, scales_ref,
    owner_ref, slot_ref, hidden_ref, gain_ref, kv_gain_ref, gain_row, load_sem,
    weights, normed, select, placing, outgoing, incoming, stats_out, stats_in,
    gain_col, hop_send, weight_recv, normed_sem, stats_sem, block_send, block_recv,
):
    group, seq, tp = lax.axis_index("group"), lax.axis_index("seq"), lax.axis_index("tp")
    n_seq = weights.shape[0]
    cols, depth = weights.shape[1:]
    rows = hidden_ref.shape[0]
    tokens = 2 * rows
    block_count = tokens // 64
    chunk = cols // 3
    z, x = seq // X_COUNT, seq % X_COUNT
    mine, middle, other = 2 * group, 1, 2 - 2 * group

    def at(z_to, x_to):
        return (group, z_to * X_COUNT + x_to, tp)

    above, below, beside = at(z + 1, x), at(z - 1, x), at(z, 1 - x)
    across, twin = (1 - group, seq, tp), (group, seq, 1 - tp)

    loads = [
        pltpu.make_async_copy(source, target, load_sem.at[index])
        for index, (source, target) in enumerate((
            (hidden_hbm, hidden_ref), (gain_hbm, gain_ref), (weight_hbm, weights.at[seq]),
            (kv_gain_hbm, kv_gain_ref), (owner_hbm, owner_ref), (slot_hbm, slot_ref),
        ))
    ]
    for load in loads:
        load.start()

    barrier = pltpu.get_barrier_semaphore()
    for step in range(1, n_seq):
        pl.semaphore_signal(
            barrier, inc=1, device_id=(group, (seq + step) % n_seq, tp), device_id_type=MESH
        )
    for peer in (across, twin):
        pl.semaphore_signal(barrier, inc=1, device_id=peer, device_id_type=MESH)

    pl.semaphore_wait(barrier, n_seq + 1)

    def piece(shard, part, direction, peer, source=None):
        lines = pl.ds(pl.multiple_of(part * chunk, chunk), chunk)
        where = weights.at[shard, lines, :]
        return pltpu.make_async_remote_copy(
            src_ref=where if source is None else source.at[lines, :],
            dst_ref=where,
            send_sem=hop_send.at[shard, part, direction],
            recv_sem=weight_recv.at[shard, part],
            device_id=peer,
            device_id_type=MESH,
        )

    def when_inside(z_at, do):
        pl.when((z_at >= 0) & (z_at < Z_COUNT))(do)

    own = seq
    for part in (mine, middle):
        when_inside(z + 1, lambda: piece(own, part, 0, above, weight_hbm).start())
        when_inside(z - 1, lambda: piece(own, part, 1, below, weight_hbm).start())
        piece(own, part, 2, beside, weight_hbm).start()

    for load in loads:
        load.wait()
    for line in range(gain_ref.shape[0]):
        gain_row[0:1, line * 128 : (line + 1) * 128] = gain_ref[line : line + 1, :].astype(
            jnp.float32
        )
    first = pl.multiple_of(tp * rows, rows)

    def norm_tile(index, carry):
        tile = hidden_ref[pl.ds(pl.multiple_of(index * 16, 16), 16), :].astype(jnp.float32)
        power = jnp.mean(tile * tile, axis=1, keepdims=True)
        out = tile * lax.rsqrt(power + EPSILON) * gain_row[0:1, :]
        normed[pl.ds(pl.multiple_of(first + index * 16, 16), 16), :] = out.astype(jnp.bfloat16)
        return carry

    lax.fori_loop(0, rows // 16, norm_tile, 0)
    half = normed.at[pl.ds(first, rows), :]
    normed_copy = pltpu.make_async_remote_copy(
        src_ref=half, dst_ref=half, send_sem=normed_sem.at[0], recv_sem=normed_sem.at[1],
        device_id=twin, device_id_type=MESH,
    )
    normed_copy.start()

    def latent_of(part):
        line = lax.broadcasted_iota(jnp.int32, (chunk, 1), 0) + part * chunk
        return line + tp * cols < LAT

    def block_copy(source, target, part, lines):
        place = pl.ds(pl.multiple_of(part * chunk, 16), lines)
        return pltpu.make_async_remote_copy(
            src_ref=outgoing.at[target, place, :], dst_ref=incoming.at[source, place, :],
            send_sem=block_send.at[target, part], recv_sem=block_recv.at[source, part],
            device_id=(group, target, tp), device_id_type=MESH,
        )

    def hand_over(values, part, lines):
        place = pl.ds(pl.multiple_of(part * chunk, 16), lines)
        for target in range(n_seq):
            outgoing[target, place, :] = jnp.dot(
                values, select[:, target * 128 : (target + 1) * 128],
                preferred_element_type=jnp.float32,
            ).astype(jnp.bfloat16)
        for step in range(1, n_seq):
            block_copy(seq, (seq + step) % n_seq, part, lines).start()
        incoming[seq, place, :] = outgoing[seq, place, :]

    def project(part, weights_ready):
        place = pl.ds(pl.multiple_of(part * chunk, chunk), chunk)
        total = jnp.zeros((chunk, tokens), jnp.float32)
        for x_at in (x, 1 - x):
            for z_at in (z, z + 1 - 2 * (z % 2), (z + 2) % Z_COUNT, Z_COUNT - 1 - z):
                shard = z_at * X_COUNT + x_at
                weights_ready(shard, z_at, x_at)
                features = pl.ds(pl.multiple_of(shard * depth, 128), depth)
                total = total + lax.dot_general(
                    weights[shard, place, :], normed[:, features], NT,
                    preferred_element_type=jnp.float32,
                )
        latent = latent_of(part)
        gained = total * gain_col[place, :]
        power = jnp.sum(jnp.where(latent, total * total, 0.0), axis=0, keepdims=True)
        latent_peak = jnp.max(jnp.where(latent, jnp.abs(gained), 0.0), axis=0, keepdims=True)
        lower = total[chunk - ROPE : chunk - rope_half, :]
        upper = total[chunk - rope_half :, :]
        turned = jnp.concatenate(
            [lower * cosine - upper * sine, upper * cosine + lower * sine], axis=0
        )
        rope_here = (tp == 1) & (part == 2)
        rope_peak = jnp.max(jnp.abs(turned), axis=0, keepdims=True)
        rope_peak = jnp.where(rope_here, rope_peak, 0.0)
        values = jnp.where(
            latent, gained, jnp.concatenate([gained[: chunk - ROPE, :], turned], axis=0)
        )
        hand_over(values.astype(jnp.bfloat16), part, chunk)
        return power, latent_peak, rope_peak

    def arrive(z_from, x_from, part, step=0):
        def do():
            shard = z_from * X_COUNT + x_from
            piece(shard, part, 2, beside).wait_recv()
            if part is mine:
                piece(shard, part, 3, across).start()
            if step == 1:
                when_inside(z + 1, lambda: piece(shard, part, 0, above).start())
            if step == -1:
                when_inside(z - 1, lambda: piece(shard, part, 1, below).start())
            if step != 0:
                piece(shard, part, 2, beside).start()
        when_inside(z_from, do)

    def arrive_column(distance, part):
        arrive(z - distance, x, part, 1)
        arrive(z + distance, x, part, -1)

    def arrive_beside(distance, part):
        arrive(z - distance, 1 - x, part)
        if distance:
            arrive(z + distance, 1 - x, part)

    arrive_column(1, mine)
    arrive_beside(0, mine)

    def rank_of(base, block):
        same = [
            jnp.where(owner_ref[base + earlier] == owner_ref[base + block], 1, 0)
            for earlier in range(block)
        ]
        return sum(same, jnp.int32(0))

    lane_id = lax.broadcasted_iota(jnp.int32, (64, n_seq * 128), 1)
    line_id = lax.broadcasted_iota(jnp.int32, (64, n_seq * 128), 0)
    for block in range(block_count):
        place = owner_ref[seq * block_count + block] * 128 + rank_of(seq * block_count, block) * 64
        select[pl.ds(block * 64, 64), :] = jnp.where(lane_id - line_id == place, 1.0, 0.0).astype(
            jnp.bfloat16
        )

    arrive_column(2, mine)
    arrive_column(1, middle)
    arrive_beside(1, mine)

    slot_total = cache_ref.shape[0] // 64
    lane_in = lax.broadcasted_iota(jnp.int32, (slot_total * 64, 128), 1)
    line_in = lax.broadcasted_iota(jnp.int32, (slot_total * 64, 128), 0)

    def slots_from(source):
        found = [jnp.int32(-1), jnp.int32(-1)]
        for block in range(block_count):
            entry = source * block_count + block
            rank = rank_of(source * block_count, block)
            for place in range(SEND_CAP):
                hit = (owner_ref[entry] == seq) & (rank == place)
                found[place] = jnp.where(hit, slot_ref[entry], found[place])
        return found

    slots = [slots_from(source) for source in range(n_seq)]
    for source in range(n_seq):
        low, high = slots[source]
        target = jnp.where(lane_in < 64, low * 64, high * 64) + lane_in % 64
        placing[:, source * 128 : (source + 1) * 128] = jnp.where(
            line_in == target, 1.0, 0.0
        ).astype(jnp.bfloat16)

    arrive_column(3, mine)
    arrive_column(2, middle)

    rope_half = ROPE // 2
    positions = lax.broadcasted_iota(jnp.int32, (rope_half, tokens), 1) + seq * tokens
    positions = positions.astype(jnp.float32)
    pair = lax.broadcasted_iota(jnp.int32, (rope_half, 1), 0)
    periods = jnp.zeros((rope_half, 1), jnp.float32)
    for index, period in enumerate(rope_periods(ROPE)):
        periods = jnp.where(pair == index, float(period), periods)
    turns = jnp.floor((positions + 0.5) / periods)
    phase = (positions - turns * periods) * (2.0 * math.pi) / periods
    cosine, sine = jnp.cos(phase), jnp.sin(phase)

    column = lax.broadcasted_iota(jnp.int32, (cols, LAT), 0) + tp * cols
    gain_lane = lax.broadcasted_iota(jnp.int32, (cols, LAT), 1)
    gain_all = jnp.concatenate(
        [kv_gain_ref[line : line + 1, :].astype(jnp.float32) for line in range(LAT // 128)], axis=1
    )
    gain_col[...] = jnp.sum(
        jnp.where(column == gain_lane, gain_all, 0.0), axis=1, keepdims=True
    )

    arrive_beside(2, mine)
    arrive_beside(3, mine)

    normed_copy.wait()
    first_stats = project(mine, lambda shard, z_at, x_at: None)

    arrive_column(3, middle)

    def by_beside(shard, z_at, x_at):
        if x_at is not x:
            piece(shard, middle, 2, beside).wait_recv()

    def by_across(shard, z_at, x_at):
        if not (z_at is z and x_at is x):
            piece(shard, other, 3, across).wait_recv()

    stats = [first_stats, project(other, by_across), project(middle, by_beside)]
    power = sum(one[0] for one in stats)
    latent_peak = functools.reduce(jnp.maximum, [one[1] for one in stats])
    rope_peak = functools.reduce(jnp.maximum, [one[2] for one in stats])

    stats_out[0:1, :] = power
    stats_out[1:2, :] = latent_peak
    stats_out[2:3, :] = rope_peak
    stats_out[3:8, :] = jnp.zeros((5, tokens), jnp.float32)
    stats_copy = pltpu.make_async_remote_copy(
        src_ref=stats_out, dst_ref=stats_in, send_sem=stats_sem.at[0], recv_sem=stats_sem.at[1],
        device_id=twin, device_id_type=MESH,
    )
    stats_copy.start()
    stats_copy.wait()
    inverse = lax.rsqrt((power + stats_in[0:1, :]) / LAT + EPSILON)
    peak = jnp.maximum(
        jnp.maximum(latent_peak, stats_in[1:2, :]) * inverse,
        jnp.maximum(rope_peak, stats_in[2:3, :]),
    )
    scale = (peak + EPSILON).astype(jnp.bfloat16).astype(jnp.float32)

    def terms(value):
        found = []
        for _ in range(3):
            term = value.astype(jnp.bfloat16).astype(jnp.float32)
            found.append(term)
            value = value - term
        return found

    lines = terms(inverse / scale) + terms(1.0 / scale) + [scale]
    lines = lines + [jnp.zeros((SCALE_ROWS - len(lines), tokens), jnp.float32)]
    hand_over(jnp.concatenate(lines, axis=0).astype(jnp.bfloat16), 3, SCALE_ROWS)

    column_id = lax.broadcasted_iota(jnp.int32, (cols, 1), 0) + tp * cols
    slot_id = lax.broadcasted_iota(jnp.int32, (slot_total, 128), 0)
    lane = lax.broadcasted_iota(jnp.int32, (slot_total, 128), 1)
    for part in (mine, other, middle):
        for step in range(1, n_seq):
            source = (seq + step) % n_seq
            block_copy(source, source, part, chunk).wait_recv()
    for step in range(1, n_seq):
        source = (seq + step) % n_seq
        block_copy(source, source, 3, SCALE_ROWS).wait_recv()
    placed = jnp.zeros((slot_total, 128), jnp.float32)
    arrived = []
    for source in range(n_seq):
        factors = incoming[source, cols : cols + SCALE_ROWS, :].astype(jnp.float32)
        latent_factor = factors[0:1, :] + factors[1:2, :] + factors[2:3, :]
        rope_factor = factors[3:4, :] + factors[4:5, :] + factors[5:6, :]
        factor = jnp.where(column_id < LAT, latent_factor, rope_factor)
        values = incoming[source, :cols, :].astype(jnp.float32)
        arrived.append((values * factor).astype(jnp.bfloat16))
        low, high = slots[source]
        hit = slot_id == jnp.where(lane < 64, low, high)
        placed = placed + jnp.where(hit, factors[6:7, :], 0.0)
    cache_ref[...] = lax.dot_general(
        placing[...], jnp.concatenate(arrived, axis=1), NT, preferred_element_type=jnp.float32
    ).astype(jnp.bfloat16)
    scales_ref[...] = (placed[:, :64] + placed[:, 64:]).astype(jnp.bfloat16)

    for step in range(1, n_seq):
        target = (seq + step) % n_seq
        for part in (mine, other, middle):
            block_copy(seq, target, part, chunk).wait_send()
        block_copy(seq, target, 3, SCALE_ROWS).wait_send()
    for part in (mine, middle):
        when_inside(z + 1, lambda: piece(own, part, 0, above, weight_hbm).wait_send())
        when_inside(z - 1, lambda: piece(own, part, 1, below, weight_hbm).wait_send())
        piece(own, part, 2, beside, weight_hbm).wait_send()

    def sent(z_from, x_from, direction, z_to, peer):
        def do():
            shard = z_from * X_COUNT + x_from
            for part in (mine, middle):
                if direction is not None:
                    when_inside(z_to, lambda: piece(shard, part, direction, peer).wait_send())
                    piece(shard, part, 2, beside).wait_send()
            piece(shard, mine, 3, across).wait_send()
        when_inside(z_from, do)

    sent(z, 1 - x, None, None, None)
    for distance in range(1, Z_COUNT):
        sent(z - distance, x, 0, z + 1, above)
        sent(z + distance, x, 1, z - 1, below)
        sent(z - distance, 1 - x, None, None, None)
        sent(z + distance, 1 - x, None, None, None)


def fused(hidden, in_gain, kv_weight, kv_gain, block_owner, block_slot):
    rows, width = hidden.shape
    depth, cols = kv_weight.shape
    n_seq = lax.axis_size("seq")
    tokens = 2 * rows
    slot_total = 2 * (tokens // 64)
    padded = cols + SCALE_ROWS
    vmem = pl.BlockSpec(memory_space=pltpu.VMEM)
    hbm = pl.BlockSpec(memory_space=pltpu.HBM)
    cache, scales = pl.pallas_call(
        fused_kernel,
        out_shape=(
            jax.ShapeDtypeStruct((slot_total * 64, cols), jnp.bfloat16),
            jax.ShapeDtypeStruct((slot_total, 64), jnp.bfloat16),
        ),
        in_specs=[hbm] * 6,
        out_specs=(vmem, vmem),
        scratch_shapes=[
            pltpu.SMEM(block_owner.shape, jnp.int32),
            pltpu.SMEM(block_slot.shape, jnp.int32),
            pltpu.VMEM((rows, width), jnp.bfloat16),
            pltpu.VMEM((width // 128, 128), jnp.bfloat16),
            pltpu.VMEM((LAT // 128, 128), jnp.bfloat16),
            pltpu.VMEM((8, width), jnp.float32),
            pltpu.SemaphoreType.DMA((6,)),
            pltpu.VMEM((n_seq, cols, depth), jnp.bfloat16),
            pltpu.VMEM((tokens, width), jnp.bfloat16),
            pltpu.VMEM((tokens, n_seq * 128), jnp.bfloat16),
            pltpu.VMEM((slot_total * 64, n_seq * 128), jnp.bfloat16),
            pltpu.VMEM((n_seq, padded, 128), jnp.bfloat16),
            pltpu.VMEM((n_seq, padded, 128), jnp.bfloat16),
            pltpu.VMEM((8, tokens), jnp.float32),
            pltpu.VMEM((8, tokens), jnp.float32),
            pltpu.VMEM((cols, 1), jnp.float32),
            pltpu.SemaphoreType.DMA((n_seq, 3, 4)),
            pltpu.SemaphoreType.DMA((n_seq, 3)),
            pltpu.SemaphoreType.DMA((2,)),
            pltpu.SemaphoreType.DMA((2,)),
            pltpu.SemaphoreType.DMA((n_seq, 4)),
            pltpu.SemaphoreType.DMA((n_seq, 4)),
        ],
        compiler_params=pltpu.CompilerParams(
            collective_id=0, has_side_effects=True, vmem_limit_bytes=64 * 1024 * 1024 - 65536
        ),
    )(
        block_owner, block_slot, hidden, in_gain.reshape(width // 128, 128), kv_weight.T,
        kv_gain.reshape(LAT // 128, 128),
    )
    return (cache.reshape(slot_total, 64, cols), scales)


def solution(mesh):
    fits = (
        mesh.shape["seq"] == X_COUNT * Z_COUNT
        and mesh.shape["group"] == 2
        and mesh.shape["tp"] == 2
    )
    return jax.shard_map(
        fused if fits else per_device,
        mesh=mesh,
        in_specs=(P(("group", "seq", "tp"), None), P(), P("seq", "tp"), P(), P(), P()),
        out_specs=(P(("group", "seq"), None, "tp"), P(("group", "seq"), None)),
        check_vma=False,
    )
```

```python
import functools
import functools
import math

import jax
import jax.numpy as jnp
import numpy as np
from jax import lax
from jax.experimental import pallas as pl
from jax.experimental.pallas import tpu as pltpu
from jax.sharding import PartitionSpec as P

LAT = 512
ROPE = 64
SEND_CAP = 2


EPSILON = 1e-06


def rope_periods(rope_width):
    return np.floor(
        2.0 * np.pi * 10000.0 ** (np.arange(rope_width // 2) * 2.0 / rope_width) + 0.5
    ).astype(np.int32)


def normalize(values, in_gain):
    wide = values.astype(jnp.float32)
    power = jnp.mean(wide * wide, axis=1, keepdims=True)
    return (wide * lax.rsqrt(power + EPSILON) * in_gain.astype(jnp.float32)).astype(jnp.bfloat16)


def shape_latent(projected, power, gain_cols, positions, col_index):
    scaled = projected * lax.rsqrt(power / LAT + EPSILON)[:, None] * gain_cols[None, :]
    periods = jnp.asarray(rope_periods(ROPE))
    phase = (
        (positions[:, None] % periods[None, :]).astype(jnp.float32)
        * (2.0 * math.pi)
        / periods.astype(jnp.float32)
    )
    cosine = jnp.cos(phase)
    sine = jnp.sin(phase)
    col_total = projected.shape[1]
    rope_tail = projected[:, col_total - ROPE :]
    lower_half = rope_tail[:, : ROPE // 2]
    upper_half = rope_tail[:, ROPE // 2 :]
    rotated = jnp.concatenate(
        [lower_half * cosine - upper_half * sine, upper_half * cosine + lower_half * sine], axis=1
    )
    rotated_full = jnp.concatenate([projected[:, : col_total - ROPE], rotated], axis=1)
    return jnp.where((col_index >= LAT)[None, :], rotated_full, scaled)


def hand_off(quant, token_scale, block_owner, block_slot):
    seq_count = lax.axis_size("seq")
    seq_index = lax.axis_index("seq")
    block_count = quant.shape[0] // 64
    col_width = quant.shape[1]
    blocks_flat = quant.reshape(block_count, 64 * col_width)
    scales_flat = token_scale.reshape(block_count, 64)
    owner_grid = block_owner.reshape(seq_count, block_count)
    slot_grid = block_slot.reshape(seq_count, block_count)
    earlier = (jnp.arange(block_count)[:, None] < jnp.arange(block_count)[None, :]).astype(
        jnp.int32
    )
    own_row = lax.dynamic_slice_in_dim(owner_grid, seq_index, 1, 0)[0]
    same_owner = (own_row[:, None] == own_row[None, :]).astype(jnp.int32)
    send_rank = jnp.sum(same_owner * earlier, axis=0)
    targets = jnp.arange(seq_count, dtype=jnp.int32)
    ranks = jnp.arange(SEND_CAP, dtype=jnp.int32)
    select = (own_row[None, None, :] == targets[:, None, None]) & (
        send_rank[None, None, :] == ranks[None, :, None]
    )
    select = select.reshape(seq_count * SEND_CAP, block_count).astype(jnp.bfloat16)
    outgoing = jnp.dot(select, blocks_flat, preferred_element_type=jnp.float32).astype(jnp.bfloat16)
    outgoing_scales = jnp.dot(select, scales_flat, preferred_element_type=jnp.float32).astype(
        jnp.bfloat16
    )
    outgoing = outgoing.reshape(seq_count, SEND_CAP * 64 * col_width)
    outgoing_scales = outgoing_scales.reshape(seq_count, SEND_CAP * 64)
    incoming, incoming_scales = (
        lax.all_to_all(outgoing, "seq", split_axis=0, concat_axis=0, tiled=True),
        lax.all_to_all(outgoing_scales, "seq", split_axis=0, concat_axis=0, tiled=True),
    )
    owned_flags = (owner_grid == seq_index).astype(jnp.int32)
    recv_rank = jnp.sum(owned_flags[:, :, None] * earlier[None, :, :], axis=1)
    slot_hits = (owned_flags[:, None, :] == 1) & (recv_rank[:, None, :] == ranks[None, :, None])
    slot_of = jnp.sum(jnp.where(slot_hits, slot_grid[:, None, :] + 1, 0), axis=2) - 1
    slot_total = 2 * block_count
    placing = (
        slot_of.reshape(-1)[None, :] == jnp.arange(slot_total, dtype=jnp.int32)[:, None]
    ).astype(jnp.bfloat16)
    owner_cache = jnp.dot(
        placing,
        incoming.reshape(seq_count * SEND_CAP, 64 * col_width),
        preferred_element_type=jnp.float32,
    )
    owner_cache = owner_cache.astype(jnp.bfloat16).reshape(slot_total, 64, col_width)
    owner_scales = jnp.dot(
        placing,
        incoming_scales.reshape(seq_count * SEND_CAP, 64),
        preferred_element_type=jnp.float32,
    )
    return (owner_cache, owner_scales.astype(jnp.bfloat16))


def per_device(hidden, in_gain, kv_weight, kv_gain, block_owner, block_slot):
    seq_index = lax.axis_index("seq")
    tp_index = lax.axis_index("tp")
    gain_full = jnp.concatenate([kv_gain.astype(jnp.float32), jnp.ones((ROPE,), jnp.float32)])
    shard_rows = lax.all_gather(hidden, "tp", axis=0, tiled=True)
    normed = normalize(shard_rows, in_gain)
    row_total = shard_rows.shape[0]
    col_half = kv_weight.shape[1]
    projected = jnp.dot(
        normed,
        lax.all_gather(kv_weight, "seq", axis=0, tiled=True),
        preferred_element_type=jnp.float32,
    )
    col_index = tp_index * col_half + jnp.arange(col_half, dtype=jnp.int32)
    latent_part = jnp.where((col_index < LAT)[None, :], projected * projected, 0.0)
    power = lax.psum(jnp.sum(latent_part, axis=1), "tp")
    gain_cols = lax.dynamic_slice_in_dim(gain_full, tp_index * col_half, col_half, 0)
    positions = seq_index * row_total + jnp.arange(row_total, dtype=jnp.int32)
    shaped = shape_latent(projected, power, gain_cols, positions, col_index)
    token_peak = lax.pmax(jnp.max(jnp.abs(shaped), axis=1), "tp")
    token_scale = (token_peak + EPSILON).astype(jnp.bfloat16)
    quant = (shaped / token_scale.astype(jnp.float32)[:, None]).astype(jnp.bfloat16)
    return hand_off(quant, token_scale, block_owner, block_slot)


MESH = pl.DeviceIdType.MESH
X_COUNT = 2
Z_COUNT = 4
NT = (((1,), (1,)), ((), ()))
SCALE_ROWS = 16


def fused_kernel(
    owner_hbm, slot_hbm, hidden_hbm, gain_hbm, weight_hbm, kv_gain_hbm,
    cache_ref, scales_ref,
    owner_ref, slot_ref, hidden_ref, gain_ref, kv_gain_ref, gain_row, load_sem,
    weights, normed, select, placing, outgoing, incoming, stats_out, stats_in,
    gain_col, in_slots, hop_send, weight_recv, normed_sem, stats_sem, block_send, block_recv,
):
    group, seq, tp = lax.axis_index("group"), lax.axis_index("seq"), lax.axis_index("tp")
    n_seq = weights.shape[0]
    cols, depth = weights.shape[1:]
    rows = hidden_ref.shape[0]
    tokens = 2 * rows
    block_count = tokens // 64
    chunk = cols // 3
    z, x = seq // X_COUNT, seq % X_COUNT
    mine, middle, other = 2 * group, 1, 2 - 2 * group

    def at(z_to, x_to):
        return (group, z_to * X_COUNT + x_to, tp)

    above, below, beside = at(z + 1, x), at(z - 1, x), at(z, 1 - x)
    across, twin = (1 - group, seq, tp), (group, seq, 1 - tp)

    loads = [
        pltpu.make_async_copy(source, target, load_sem.at[index])
        for index, (source, target) in enumerate((
            (hidden_hbm, hidden_ref), (gain_hbm, gain_ref), (weight_hbm, weights.at[seq]),
            (kv_gain_hbm, kv_gain_ref), (owner_hbm, owner_ref), (slot_hbm, slot_ref),
        ))
    ]
    for load in loads:
        load.start()

    barrier = pltpu.get_barrier_semaphore()
    for step in range(1, n_seq):
        pl.semaphore_signal(
            barrier, inc=1, device_id=(group, (seq + step) % n_seq, tp), device_id_type=MESH
        )
    for peer in (across, twin):
        pl.semaphore_signal(barrier, inc=1, device_id=peer, device_id_type=MESH)

    pl.semaphore_wait(barrier, n_seq + 1)

    def piece(shard, part, direction, peer, source=None):
        lines = pl.ds(pl.multiple_of(part * chunk, chunk), chunk)
        where = weights.at[shard, lines, :]
        return pltpu.make_async_remote_copy(
            src_ref=where if source is None else source.at[lines, :],
            dst_ref=where,
            send_sem=hop_send.at[shard, part, direction],
            recv_sem=weight_recv.at[shard, part],
            device_id=peer,
            device_id_type=MESH,
        )

    def when_inside(z_at, do):
        pl.when((z_at >= 0) & (z_at < Z_COUNT))(do)

    own = seq
    for part in (mine, middle):
        when_inside(z + 1, lambda: piece(own, part, 0, above, weight_hbm).start())
        when_inside(z - 1, lambda: piece(own, part, 1, below, weight_hbm).start())
        piece(own, part, 2, beside, weight_hbm).start()

    for load in loads:
        load.wait()
    for line in range(gain_ref.shape[0]):
        gain_row[0:1, line * 128 : (line + 1) * 128] = gain_ref[line : line + 1, :].astype(
            jnp.float32
        )
    first = pl.multiple_of(tp * rows, rows)

    def norm_tile(index, carry):
        tile = hidden_ref[pl.ds(pl.multiple_of(index * 16, 16), 16), :].astype(jnp.float32)
        power = jnp.mean(tile * tile, axis=1, keepdims=True)
        out = tile * lax.rsqrt(power + EPSILON) * gain_row[0:1, :]
        normed[pl.ds(pl.multiple_of(first + index * 16, 16), 16), :] = out.astype(jnp.bfloat16)
        return carry

    lax.fori_loop(0, rows // 16, norm_tile, 0)
    half = normed.at[pl.ds(first, rows), :]
    normed_copy = pltpu.make_async_remote_copy(
        src_ref=half, dst_ref=half, send_sem=normed_sem.at[0], recv_sem=normed_sem.at[1],
        device_id=twin, device_id_type=MESH,
    )
    normed_copy.start()

    def latent_of(part):
        line = lax.broadcasted_iota(jnp.int32, (chunk, 1), 0) + part * chunk
        return line + tp * cols < LAT

    def block_copy(source, target, part, lines):
        place = pl.ds(pl.multiple_of(part * chunk, 16), lines)
        return pltpu.make_async_remote_copy(
            src_ref=outgoing.at[target, place, :], dst_ref=incoming.at[source, place, :],
            send_sem=block_send.at[target, part], recv_sem=block_recv.at[source, part],
            device_id=(group, target, tp), device_id_type=MESH,
        )

    def hand_over(values, part, lines):
        place = pl.ds(pl.multiple_of(part * chunk, 16), lines)
        for target in range(n_seq):
            outgoing[target, place, :] = jnp.dot(
                values, select[:, target * 128 : (target + 1) * 128],
                preferred_element_type=jnp.float32,
            ).astype(jnp.bfloat16)
        for step in range(1, n_seq):
            block_copy(seq, (seq + step) % n_seq, part, lines).start()
        incoming[seq, place, :] = outgoing[seq, place, :]

    def project(part, weights_ready):
        place = pl.ds(pl.multiple_of(part * chunk, chunk), chunk)
        total = jnp.zeros((chunk, tokens), jnp.float32)
        for x_at in (x, 1 - x):
            for z_at in (z, z + 1 - 2 * (z % 2), (z + 2) % Z_COUNT, Z_COUNT - 1 - z):
                shard = z_at * X_COUNT + x_at
                weights_ready(shard, z_at, x_at)
                features = pl.ds(pl.multiple_of(shard * depth, 128), depth)
                total = total + lax.dot_general(
                    weights[shard, place, :], normed[:, features], NT,
                    preferred_element_type=jnp.float32,
                )
        latent = latent_of(part)
        gained = total * gain_col[place, :]
        power = jnp.sum(jnp.where(latent, total * total, 0.0), axis=0, keepdims=True)
        latent_peak = jnp.max(jnp.where(latent, jnp.abs(gained), 0.0), axis=0, keepdims=True)
        lower = total[chunk - ROPE : chunk - rope_half, :]
        upper = total[chunk - rope_half :, :]
        turned = jnp.concatenate(
            [lower * cosine - upper * sine, upper * cosine + lower * sine], axis=0
        )
        rope_here = (tp == 1) & (part == 2)
        rope_peak = jnp.max(jnp.abs(turned), axis=0, keepdims=True)
        rope_peak = jnp.where(rope_here, rope_peak, 0.0)
        values = jnp.where(
            latent, gained, jnp.concatenate([gained[: chunk - ROPE, :], turned], axis=0)
        )
        hand_over(values.astype(jnp.bfloat16), part, chunk)
        return power, latent_peak, rope_peak

    def arrive(z_from, x_from, part, step=0):
        def do():
            shard = z_from * X_COUNT + x_from
            piece(shard, part, 2, beside).wait_recv()
            if part is mine:
                piece(shard, part, 3, across).start()
            if step == 1:
                when_inside(z + 1, lambda: piece(shard, part, 0, above).start())
            if step == -1:
                when_inside(z - 1, lambda: piece(shard, part, 1, below).start())
            if step != 0:
                piece(shard, part, 2, beside).start()
        when_inside(z_from, do)

    def arrive_column(distance, part):
        arrive(z - distance, x, part, 1)
        arrive(z + distance, x, part, -1)

    def arrive_beside(distance, part):
        arrive(z - distance, 1 - x, part)
        if distance:
            arrive(z + distance, 1 - x, part)

    arrive_column(1, mine)
    arrive_beside(0, mine)

    def rank_of(base, block):
        same = [
            jnp.where(owner_ref[base + earlier] == owner_ref[base + block], 1, 0)
            for earlier in range(block)
        ]
        return sum(same, jnp.int32(0))

    lane_id = lax.broadcasted_iota(jnp.int32, (64, n_seq * 128), 1)
    line_id = lax.broadcasted_iota(jnp.int32, (64, n_seq * 128), 0)
    for block in range(block_count):
        place = owner_ref[seq * block_count + block] * 128 + rank_of(seq * block_count, block) * 64
        select[pl.ds(block * 64, 64), :] = jnp.where(lane_id - line_id == place, 1.0, 0.0).astype(
            jnp.bfloat16
        )

    arrive_column(2, mine)
    arrive_column(1, middle)
    arrive_beside(1, mine)

    slot_total = cache_ref.shape[0] // 64
    lane_in = lax.broadcasted_iota(jnp.int32, (slot_total * 64, 128), 1)
    line_in = lax.broadcasted_iota(jnp.int32, (slot_total * 64, 128), 0)

    def slots_from(source):
        found = [jnp.int32(-1), jnp.int32(-1)]
        for block in range(block_count):
            entry = source * block_count + block
            rank = rank_of(source * block_count, block)
            for place in range(SEND_CAP):
                hit = (owner_ref[entry] == seq) & (rank == place)
                found[place] = jnp.where(hit, slot_ref[entry], found[place])
        return found

    slots = [slots_from(source) for source in range(n_seq)]
    for source in range(n_seq):
        low, high = slots[source]
        target = jnp.where(lane_in < 64, low * 64, high * 64) + lane_in % 64
        placing[:, source * 128 : (source + 1) * 128] = jnp.where(
            line_in == target, 1.0, 0.0
        ).astype(jnp.bfloat16)

    arrive_column(3, mine)
    arrive_column(2, middle)

    rope_half = ROPE // 2
    positions = lax.broadcasted_iota(jnp.int32, (rope_half, tokens), 1) + seq * tokens
    positions = positions.astype(jnp.float32)
    pair = lax.broadcasted_iota(jnp.int32, (rope_half, 1), 0)
    periods = jnp.zeros((rope_half, 1), jnp.float32)
    for index, period in enumerate(rope_periods(ROPE)):
        periods = jnp.where(pair == index, float(period), periods)
    turns = jnp.floor((positions + 0.5) / periods)
    phase = (positions - turns * periods) * (2.0 * math.pi) / periods
    cosine, sine = jnp.cos(phase), jnp.sin(phase)

    column = lax.broadcasted_iota(jnp.int32, (cols, LAT), 0) + tp * cols
    gain_lane = lax.broadcasted_iota(jnp.int32, (cols, LAT), 1)
    gain_all = jnp.concatenate(
        [kv_gain_ref[line : line + 1, :].astype(jnp.float32) for line in range(LAT // 128)], axis=1
    )
    gain_col[...] = jnp.sum(
        jnp.where(column == gain_lane, gain_all, 0.0), axis=1, keepdims=True
    )

    arrive_beside(2, mine)
    arrive_beside(3, mine)

    normed_copy.wait()
    first_stats = project(mine, lambda shard, z_at, x_at: None)

    arrive_column(3, middle)

    def by_beside(shard, z_at, x_at):
        if x_at is not x:
            piece(shard, middle, 2, beside).wait_recv()

    def by_across(shard, z_at, x_at):
        if not (z_at is z and x_at is x):
            piece(shard, other, 3, across).wait_recv()

    stats = [first_stats, project(other, by_across), project(middle, by_beside)]
    power = sum(one[0] for one in stats)
    latent_peak = functools.reduce(jnp.maximum, [one[1] for one in stats])
    rope_peak = functools.reduce(jnp.maximum, [one[2] for one in stats])

    def place_chunk(part):
        lines = pl.ds(pl.multiple_of(part * chunk, chunk), chunk)
        for step in range(1, n_seq):
            source = (seq + step) % n_seq
            block_copy(source, source, part, chunk).wait_recv()
        arrived = jnp.concatenate([incoming[source, lines, :] for source in range(n_seq)], axis=1)
        in_slots[part] = lax.dot_general(
            placing[...], arrived, NT, preferred_element_type=jnp.float32
        )

    stats_out[0:1, :] = power
    stats_out[1:2, :] = latent_peak
    stats_out[2:3, :] = rope_peak
    stats_out[3:8, :] = jnp.zeros((5, tokens), jnp.float32)
    stats_copy = pltpu.make_async_remote_copy(
        src_ref=stats_out, dst_ref=stats_in, send_sem=stats_sem.at[0], recv_sem=stats_sem.at[1],
        device_id=twin, device_id_type=MESH,
    )
    stats_copy.start()
    place_chunk(mine)
    stats_copy.wait()
    inverse = lax.rsqrt((power + stats_in[0:1, :]) / LAT + EPSILON)
    peak = jnp.maximum(
        jnp.maximum(latent_peak, stats_in[1:2, :]) * inverse,
        jnp.maximum(rope_peak, stats_in[2:3, :]),
    )
    scale = (peak + EPSILON).astype(jnp.bfloat16).astype(jnp.float32)

    def terms(value):
        found = []
        for _ in range(3):
            term = value.astype(jnp.bfloat16).astype(jnp.float32)
            found.append(term)
            value = value - term
        return found

    lines = terms(inverse / scale) + terms(1.0 / scale) + [scale]
    lines = lines + [jnp.zeros((SCALE_ROWS - len(lines), tokens), jnp.float32)]
    hand_over(jnp.concatenate(lines, axis=0).astype(jnp.bfloat16), 3, SCALE_ROWS)

    place_chunk(other)
    place_chunk(middle)

    slot_id = lax.broadcasted_iota(jnp.int32, (slot_total, 128), 0)
    lane = lax.broadcasted_iota(jnp.int32, (slot_total, 128), 1)
    for step in range(1, n_seq):
        source = (seq + step) % n_seq
        block_copy(source, source, 3, SCALE_ROWS).wait_recv()
    factors = jnp.concatenate(
        [incoming[source, cols : cols + SCALE_ROWS, :] for source in range(n_seq)], axis=1
    )
    by_row = lax.dot_general(placing[...], factors, NT, preferred_element_type=jnp.float32)
    latent_factor = by_row[:, 0:1] + by_row[:, 1:2] + by_row[:, 2:3]
    rope_factor = by_row[:, 3:4] + by_row[:, 4:5] + by_row[:, 5:6]
    column_id = lax.broadcasted_iota(jnp.int32, (1, cols), 1) + tp * cols
    factor = jnp.where(column_id < LAT, latent_factor, rope_factor)
    values = jnp.concatenate([in_slots[part] for part in range(3)], axis=1)
    cache_ref[...] = (values * factor).astype(jnp.bfloat16)
    placed = jnp.zeros((slot_total, 128), jnp.float32)
    for source in range(n_seq):
        low, high = slots[source]
        hit = slot_id == jnp.where(lane < 64, low, high)
        scales_in = incoming[source, cols : cols + SCALE_ROWS, :].astype(jnp.float32)
        placed = placed + jnp.where(hit, scales_in[6:7, :], 0.0)
    scales_ref[...] = (placed[:, :64] + placed[:, 64:]).astype(jnp.bfloat16)

    for step in range(1, n_seq):
        target = (seq + step) % n_seq
        for part in (mine, other, middle):
            block_copy(seq, target, part, chunk).wait_send()
        block_copy(seq, target, 3, SCALE_ROWS).wait_send()
    for part in (mine, middle):
        when_inside(z + 1, lambda: piece(own, part, 0, above, weight_hbm).wait_send())
        when_inside(z - 1, lambda: piece(own, part, 1, below, weight_hbm).wait_send())
        piece(own, part, 2, beside, weight_hbm).wait_send()

    def sent(z_from, x_from, direction, z_to, peer):
        def do():
            shard = z_from * X_COUNT + x_from
            for part in (mine, middle):
                if direction is not None:
                    when_inside(z_to, lambda: piece(shard, part, direction, peer).wait_send())
                    piece(shard, part, 2, beside).wait_send()
            piece(shard, mine, 3, across).wait_send()
        when_inside(z_from, do)

    sent(z, 1 - x, None, None, None)
    for distance in range(1, Z_COUNT):
        sent(z - distance, x, 0, z + 1, above)
        sent(z + distance, x, 1, z - 1, below)
        sent(z - distance, 1 - x, None, None, None)
        sent(z + distance, 1 - x, None, None, None)


def fused(hidden, in_gain, kv_weight, kv_gain, block_owner, block_slot):
    rows, width = hidden.shape
    depth, cols = kv_weight.shape
    n_seq = lax.axis_size("seq")
    tokens = 2 * rows
    slot_total = 2 * (tokens // 64)
    padded = cols + SCALE_ROWS
    vmem = pl.BlockSpec(memory_space=pltpu.VMEM)
    hbm = pl.BlockSpec(memory_space=pltpu.HBM)
    cache, scales = pl.pallas_call(
        fused_kernel,
        out_shape=(
            jax.ShapeDtypeStruct((slot_total * 64, cols), jnp.bfloat16),
            jax.ShapeDtypeStruct((slot_total, 64), jnp.bfloat16),
        ),
        in_specs=[hbm] * 6,
        out_specs=(vmem, vmem),
        scratch_shapes=[
            pltpu.SMEM(block_owner.shape, jnp.int32),
            pltpu.SMEM(block_slot.shape, jnp.int32),
            pltpu.VMEM((rows, width), jnp.bfloat16),
            pltpu.VMEM((width // 128, 128), jnp.bfloat16),
            pltpu.VMEM((LAT // 128, 128), jnp.bfloat16),
            pltpu.VMEM((8, width), jnp.float32),
            pltpu.SemaphoreType.DMA((6,)),
            pltpu.VMEM((n_seq, cols, depth), jnp.bfloat16),
            pltpu.VMEM((tokens, width), jnp.bfloat16),
            pltpu.VMEM((tokens, n_seq * 128), jnp.bfloat16),
            pltpu.VMEM((slot_total * 64, n_seq * 128), jnp.bfloat16),
            pltpu.VMEM((n_seq, padded, 128), jnp.bfloat16),
            pltpu.VMEM((n_seq, padded, 128), jnp.bfloat16),
            pltpu.VMEM((8, tokens), jnp.float32),
            pltpu.VMEM((8, tokens), jnp.float32),
            pltpu.VMEM((cols, 1), jnp.float32),
            pltpu.VMEM((3, slot_total * 64, cols // 3), jnp.float32),
            pltpu.SemaphoreType.DMA((n_seq, 3, 4)),
            pltpu.SemaphoreType.DMA((n_seq, 3)),
            pltpu.SemaphoreType.DMA((2,)),
            pltpu.SemaphoreType.DMA((2,)),
            pltpu.SemaphoreType.DMA((n_seq, 4)),
            pltpu.SemaphoreType.DMA((n_seq, 4)),
        ],
        compiler_params=pltpu.CompilerParams(
            collective_id=0, has_side_effects=True, vmem_limit_bytes=64 * 1024 * 1024 - 65536
        ),
    )(
        block_owner, block_slot, hidden, in_gain.reshape(width // 128, 128), kv_weight.T,
        kv_gain.reshape(LAT // 128, 128),
    )
    return (cache.reshape(slot_total, 64, cols), scales)


def solution(mesh):
    fits = (
        mesh.shape["seq"] == X_COUNT * Z_COUNT
        and mesh.shape["group"] == 2
        and mesh.shape["tp"] == 2
    )
    return jax.shard_map(
        fused if fits else per_device,
        mesh=mesh,
        in_specs=(P(("group", "seq", "tp"), None), P(), P("seq", "tp"), P(), P(), P()),
        out_specs=(P(("group", "seq"), None, "tp"), P(("group", "seq"), None)),
        check_vma=False,
    )
```

```python
import functools
import functools
import math

import jax
import jax.numpy as jnp
import numpy as np
from jax import lax
from jax.experimental import pallas as pl
from jax.experimental.pallas import tpu as pltpu
from jax.sharding import PartitionSpec as P

LAT = 512
ROPE = 64
SEND_CAP = 2


EPSILON = 1e-06


def rope_periods(rope_width):
    return np.floor(
        2.0 * np.pi * 10000.0 ** (np.arange(rope_width // 2) * 2.0 / rope_width) + 0.5
    ).astype(np.int32)


def normalize(values, in_gain):
    wide = values.astype(jnp.float32)
    power = jnp.mean(wide * wide, axis=1, keepdims=True)
    return (wide * lax.rsqrt(power + EPSILON) * in_gain.astype(jnp.float32)).astype(jnp.bfloat16)


def shape_latent(projected, power, gain_cols, positions, col_index):
    scaled = projected * lax.rsqrt(power / LAT + EPSILON)[:, None] * gain_cols[None, :]
    periods = jnp.asarray(rope_periods(ROPE))
    phase = (
        (positions[:, None] % periods[None, :]).astype(jnp.float32)
        * (2.0 * math.pi)
        / periods.astype(jnp.float32)
    )
    cosine = jnp.cos(phase)
    sine = jnp.sin(phase)
    col_total = projected.shape[1]
    rope_tail = projected[:, col_total - ROPE :]
    lower_half = rope_tail[:, : ROPE // 2]
    upper_half = rope_tail[:, ROPE // 2 :]
    rotated = jnp.concatenate(
        [lower_half * cosine - upper_half * sine, upper_half * cosine + lower_half * sine], axis=1
    )
    rotated_full = jnp.concatenate([projected[:, : col_total - ROPE], rotated], axis=1)
    return jnp.where((col_index >= LAT)[None, :], rotated_full, scaled)


def hand_off(quant, token_scale, block_owner, block_slot):
    seq_count = lax.axis_size("seq")
    seq_index = lax.axis_index("seq")
    block_count = quant.shape[0] // 64
    col_width = quant.shape[1]
    blocks_flat = quant.reshape(block_count, 64 * col_width)
    scales_flat = token_scale.reshape(block_count, 64)
    owner_grid = block_owner.reshape(seq_count, block_count)
    slot_grid = block_slot.reshape(seq_count, block_count)
    earlier = (jnp.arange(block_count)[:, None] < jnp.arange(block_count)[None, :]).astype(
        jnp.int32
    )
    own_row = lax.dynamic_slice_in_dim(owner_grid, seq_index, 1, 0)[0]
    same_owner = (own_row[:, None] == own_row[None, :]).astype(jnp.int32)
    send_rank = jnp.sum(same_owner * earlier, axis=0)
    targets = jnp.arange(seq_count, dtype=jnp.int32)
    ranks = jnp.arange(SEND_CAP, dtype=jnp.int32)
    select = (own_row[None, None, :] == targets[:, None, None]) & (
        send_rank[None, None, :] == ranks[None, :, None]
    )
    select = select.reshape(seq_count * SEND_CAP, block_count).astype(jnp.bfloat16)
    outgoing = jnp.dot(select, blocks_flat, preferred_element_type=jnp.float32).astype(jnp.bfloat16)
    outgoing_scales = jnp.dot(select, scales_flat, preferred_element_type=jnp.float32).astype(
        jnp.bfloat16
    )
    outgoing = outgoing.reshape(seq_count, SEND_CAP * 64 * col_width)
    outgoing_scales = outgoing_scales.reshape(seq_count, SEND_CAP * 64)
    incoming, incoming_scales = (
        lax.all_to_all(outgoing, "seq", split_axis=0, concat_axis=0, tiled=True),
        lax.all_to_all(outgoing_scales, "seq", split_axis=0, concat_axis=0, tiled=True),
    )
    owned_flags = (owner_grid == seq_index).astype(jnp.int32)
    recv_rank = jnp.sum(owned_flags[:, :, None] * earlier[None, :, :], axis=1)
    slot_hits = (owned_flags[:, None, :] == 1) & (recv_rank[:, None, :] == ranks[None, :, None])
    slot_of = jnp.sum(jnp.where(slot_hits, slot_grid[:, None, :] + 1, 0), axis=2) - 1
    slot_total = 2 * block_count
    placing = (
        slot_of.reshape(-1)[None, :] == jnp.arange(slot_total, dtype=jnp.int32)[:, None]
    ).astype(jnp.bfloat16)
    owner_cache = jnp.dot(
        placing,
        incoming.reshape(seq_count * SEND_CAP, 64 * col_width),
        preferred_element_type=jnp.float32,
    )
    owner_cache = owner_cache.astype(jnp.bfloat16).reshape(slot_total, 64, col_width)
    owner_scales = jnp.dot(
        placing,
        incoming_scales.reshape(seq_count * SEND_CAP, 64),
        preferred_element_type=jnp.float32,
    )
    return (owner_cache, owner_scales.astype(jnp.bfloat16))


def per_device(hidden, in_gain, kv_weight, kv_gain, block_owner, block_slot):
    seq_index = lax.axis_index("seq")
    tp_index = lax.axis_index("tp")
    gain_full = jnp.concatenate([kv_gain.astype(jnp.float32), jnp.ones((ROPE,), jnp.float32)])
    shard_rows = lax.all_gather(hidden, "tp", axis=0, tiled=True)
    normed = normalize(shard_rows, in_gain)
    row_total = shard_rows.shape[0]
    col_half = kv_weight.shape[1]
    projected = jnp.dot(
        normed,
        lax.all_gather(kv_weight, "seq", axis=0, tiled=True),
        preferred_element_type=jnp.float32,
    )
    col_index = tp_index * col_half + jnp.arange(col_half, dtype=jnp.int32)
    latent_part = jnp.where((col_index < LAT)[None, :], projected * projected, 0.0)
    power = lax.psum(jnp.sum(latent_part, axis=1), "tp")
    gain_cols = lax.dynamic_slice_in_dim(gain_full, tp_index * col_half, col_half, 0)
    positions = seq_index * row_total + jnp.arange(row_total, dtype=jnp.int32)
    shaped = shape_latent(projected, power, gain_cols, positions, col_index)
    token_peak = lax.pmax(jnp.max(jnp.abs(shaped), axis=1), "tp")
    token_scale = (token_peak + EPSILON).astype(jnp.bfloat16)
    quant = (shaped / token_scale.astype(jnp.float32)[:, None]).astype(jnp.bfloat16)
    return hand_off(quant, token_scale, block_owner, block_slot)


MESH = pl.DeviceIdType.MESH
X_COUNT = 2
Z_COUNT = 4
NT = (((1,), (1,)), ((), ()))
SCALE_ROWS = 16


def fused_kernel(
    owner_hbm, slot_hbm, hidden_hbm, gain_hbm, weight_hbm, kv_gain_hbm,
    cache_ref, scales_ref,
    owner_ref, slot_ref, hidden_ref, gain_ref, kv_gain_ref, gain_row, load_sem,
    weights, normed, select, placing, outgoing, incoming, stats_out, stats_in,
    gain_col, in_slots, hop_send, weight_recv, normed_sem, stats_sem, block_send, block_recv,
):
    group, seq, tp = lax.axis_index("group"), lax.axis_index("seq"), lax.axis_index("tp")
    n_seq = weights.shape[0]
    cols, depth = weights.shape[1:]
    rows = hidden_ref.shape[0]
    tokens = 2 * rows
    block_count = tokens // 64
    chunk = cols // 3
    z, x = seq // X_COUNT, seq % X_COUNT
    mine, middle, other = 2 * group, 1, 2 - 2 * group

    def at(z_to, x_to):
        return (group, z_to * X_COUNT + x_to, tp)

    above, below, beside = at(z + 1, x), at(z - 1, x), at(z, 1 - x)
    across, twin = (1 - group, seq, tp), (group, seq, 1 - tp)

    loads = [
        pltpu.make_async_copy(source, target, load_sem.at[index])
        for index, (source, target) in enumerate((
            (hidden_hbm, hidden_ref), (gain_hbm, gain_ref), (weight_hbm, weights.at[seq]),
            (kv_gain_hbm, kv_gain_ref), (owner_hbm, owner_ref), (slot_hbm, slot_ref),
        ))
    ]
    barrier = pltpu.get_barrier_semaphore()
    for step in range(1, n_seq):
        pl.semaphore_signal(
            barrier, inc=1, device_id=(group, (seq + step) % n_seq, tp), device_id_type=MESH
        )
    for peer in (across, twin):
        pl.semaphore_signal(barrier, inc=1, device_id=peer, device_id_type=MESH)

    for load in loads:
        load.start()
    pl.semaphore_wait(barrier, n_seq + 1)

    def piece(shard, part, direction, peer, source=None):
        lines = pl.ds(pl.multiple_of(part * chunk, chunk), chunk)
        where = weights.at[shard, lines, :]
        return pltpu.make_async_remote_copy(
            src_ref=where if source is None else source.at[lines, :],
            dst_ref=where,
            send_sem=hop_send.at[shard, part, direction],
            recv_sem=weight_recv.at[shard, part],
            device_id=peer,
            device_id_type=MESH,
        )

    def when_inside(z_at, do):
        pl.when((z_at >= 0) & (z_at < Z_COUNT))(do)

    own = seq
    for part in (mine, middle):
        when_inside(z + 1, lambda: piece(own, part, 0, above, weight_hbm).start())
        when_inside(z - 1, lambda: piece(own, part, 1, below, weight_hbm).start())
        piece(own, part, 2, beside, weight_hbm).start()

    for load in loads:
        load.wait()
    for line in range(gain_ref.shape[0]):
        gain_row[0:1, line * 128 : (line + 1) * 128] = gain_ref[line : line + 1, :].astype(
            jnp.float32
        )
    first = pl.multiple_of(tp * rows, rows)

    def norm_tile(index, carry):
        tile = hidden_ref[pl.ds(pl.multiple_of(index * 16, 16), 16), :].astype(jnp.float32)
        power = jnp.mean(tile * tile, axis=1, keepdims=True)
        out = tile * lax.rsqrt(power + EPSILON) * gain_row[0:1, :]
        normed[pl.ds(pl.multiple_of(first + index * 16, 16), 16), :] = out.astype(jnp.bfloat16)
        return carry

    lax.fori_loop(0, rows // 16, norm_tile, 0)
    half = normed.at[pl.ds(first, rows), :]
    normed_copy = pltpu.make_async_remote_copy(
        src_ref=half, dst_ref=half, send_sem=normed_sem.at[0], recv_sem=normed_sem.at[1],
        device_id=twin, device_id_type=MESH,
    )
    normed_copy.start()

    def latent_of(part):
        line = lax.broadcasted_iota(jnp.int32, (chunk, 1), 0) + part * chunk
        return line + tp * cols < LAT

    def block_copy(source, target, part, lines):
        place = pl.ds(pl.multiple_of(part * chunk, 16), lines)
        return pltpu.make_async_remote_copy(
            src_ref=outgoing.at[target, place, :], dst_ref=incoming.at[source, place, :],
            send_sem=block_send.at[target, part], recv_sem=block_recv.at[source, part],
            device_id=(group, target, tp), device_id_type=MESH,
        )

    def hand_over(values, part, lines):
        place = pl.ds(pl.multiple_of(part * chunk, 16), lines)
        for target in range(n_seq):
            outgoing[target, place, :] = jnp.dot(
                values, select[:, target * 128 : (target + 1) * 128],
                preferred_element_type=jnp.float32,
            ).astype(jnp.bfloat16)
        for step in range(1, n_seq):
            block_copy(seq, (seq + step) % n_seq, part, lines).start()
        incoming[seq, place, :] = outgoing[seq, place, :]

    def project(part, weights_ready):
        place = pl.ds(pl.multiple_of(part * chunk, chunk), chunk)
        total = jnp.zeros((chunk, tokens), jnp.float32)
        for x_at in (x, 1 - x):
            for z_at in (z, z + 1 - 2 * (z % 2), (z + 2) % Z_COUNT, Z_COUNT - 1 - z):
                shard = z_at * X_COUNT + x_at
                weights_ready(shard, z_at, x_at)
                features = pl.ds(pl.multiple_of(shard * depth, 128), depth)
                total = total + lax.dot_general(
                    weights[shard, place, :], normed[:, features], NT,
                    preferred_element_type=jnp.float32,
                )
        latent = latent_of(part)
        gained = total * gain_col[place, :]
        power = jnp.sum(jnp.where(latent, total * total, 0.0), axis=0, keepdims=True)
        latent_peak = jnp.max(jnp.where(latent, jnp.abs(gained), 0.0), axis=0, keepdims=True)
        lower = total[chunk - ROPE : chunk - rope_half, :]
        upper = total[chunk - rope_half :, :]
        turned = jnp.concatenate(
            [lower * cosine - upper * sine, upper * cosine + lower * sine], axis=0
        )
        rope_here = (tp == 1) & (part == 2)
        rope_peak = jnp.max(jnp.abs(turned), axis=0, keepdims=True)
        rope_peak = jnp.where(rope_here, rope_peak, 0.0)
        values = jnp.where(
            latent, gained, jnp.concatenate([gained[: chunk - ROPE, :], turned], axis=0)
        )
        hand_over(values.astype(jnp.bfloat16), part, chunk)
        return power, latent_peak, rope_peak

    def arrive(z_from, x_from, part, step=0):
        def do():
            shard = z_from * X_COUNT + x_from
            piece(shard, part, 2, beside).wait_recv()
            if part is mine:
                piece(shard, part, 3, across).start()
            if step == 1:
                when_inside(z + 1, lambda: piece(shard, part, 0, above).start())
            if step == -1:
                when_inside(z - 1, lambda: piece(shard, part, 1, below).start())
            if step != 0:
                piece(shard, part, 2, beside).start()
        when_inside(z_from, do)

    def arrive_column(distance, part):
        arrive(z - distance, x, part, 1)
        arrive(z + distance, x, part, -1)

    def arrive_beside(distance, part):
        arrive(z - distance, 1 - x, part)
        if distance:
            arrive(z + distance, 1 - x, part)

    arrive_column(1, mine)
    arrive_beside(0, mine)

    def rank_of(base, block):
        same = [
            jnp.where(owner_ref[base + earlier] == owner_ref[base + block], 1, 0)
            for earlier in range(block)
        ]
        return sum(same, jnp.int32(0))

    lane_id = lax.broadcasted_iota(jnp.int32, (64, n_seq * 128), 1)
    line_id = lax.broadcasted_iota(jnp.int32, (64, n_seq * 128), 0)
    for block in range(block_count):
        place = owner_ref[seq * block_count + block] * 128 + rank_of(seq * block_count, block) * 64
        select[pl.ds(block * 64, 64), :] = jnp.where(lane_id - line_id == place, 1.0, 0.0).astype(
            jnp.bfloat16
        )

    arrive_column(2, mine)
    arrive_column(1, middle)
    arrive_beside(1, mine)

    slot_total = cache_ref.shape[0] // 64
    lane_in = lax.broadcasted_iota(jnp.int32, (slot_total * 64, 128), 1)
    line_in = lax.broadcasted_iota(jnp.int32, (slot_total * 64, 128), 0)

    def slots_from(source):
        found = [jnp.int32(-1), jnp.int32(-1)]
        for block in range(block_count):
            entry = source * block_count + block
            rank = rank_of(source * block_count, block)
            for place in range(SEND_CAP):
                hit = (owner_ref[entry] == seq) & (rank == place)
                found[place] = jnp.where(hit, slot_ref[entry], found[place])
        return found

    slots = [slots_from(source) for source in range(n_seq)]
    for source in range(n_seq):
        low, high = slots[source]
        target = jnp.where(lane_in < 64, low * 64, high * 64) + lane_in % 64
        placing[:, source * 128 : (source + 1) * 128] = jnp.where(
            line_in == target, 1.0, 0.0
        ).astype(jnp.bfloat16)

    arrive_column(3, mine)
    arrive_column(2, middle)

    rope_half = ROPE // 2
    positions = lax.broadcasted_iota(jnp.int32, (rope_half, tokens), 1) + seq * tokens
    positions = positions.astype(jnp.float32)
    pair = lax.broadcasted_iota(jnp.int32, (rope_half, 1), 0)
    periods = jnp.zeros((rope_half, 1), jnp.float32)
    for index, period in enumerate(rope_periods(ROPE)):
        periods = jnp.where(pair == index, float(period), periods)
    turns = jnp.floor((positions + 0.5) / periods)
    phase = (positions - turns * periods) * (2.0 * math.pi) / periods
    cosine, sine = jnp.cos(phase), jnp.sin(phase)

    column = lax.broadcasted_iota(jnp.int32, (cols, LAT), 0) + tp * cols
    gain_lane = lax.broadcasted_iota(jnp.int32, (cols, LAT), 1)
    gain_all = jnp.concatenate(
        [kv_gain_ref[line : line + 1, :].astype(jnp.float32) for line in range(LAT // 128)], axis=1
    )
    gain_col[...] = jnp.sum(
        jnp.where(column == gain_lane, gain_all, 0.0), axis=1, keepdims=True
    )

    arrive_beside(2, mine)
    arrive_beside(3, mine)

    normed_copy.wait()
    first_stats = project(mine, lambda shard, z_at, x_at: None)

    arrive_column(3, middle)

    def by_beside(shard, z_at, x_at):
        if x_at is not x:
            piece(shard, middle, 2, beside).wait_recv()

    def by_across(shard, z_at, x_at):
        if not (z_at is z and x_at is x):
            piece(shard, other, 3, across).wait_recv()

    stats = [first_stats, project(other, by_across), project(middle, by_beside)]
    power = sum(one[0] for one in stats)
    latent_peak = functools.reduce(jnp.maximum, [one[1] for one in stats])
    rope_peak = functools.reduce(jnp.maximum, [one[2] for one in stats])

    def place_chunk(part):
        lines = pl.ds(pl.multiple_of(part * chunk, chunk), chunk)
        for step in range(1, n_seq):
            source = (seq + step) % n_seq
            block_copy(source, source, part, chunk).wait_recv()
        arrived = jnp.concatenate([incoming[source, lines, :] for source in range(n_seq)], axis=1)
        in_slots[part] = lax.dot_general(
            placing[...], arrived, NT, preferred_element_type=jnp.float32
        )

    stats_out[0:1, :] = power
    stats_out[1:2, :] = latent_peak
    stats_out[2:3, :] = rope_peak
    stats_out[3:8, :] = jnp.zeros((5, tokens), jnp.float32)
    stats_copy = pltpu.make_async_remote_copy(
        src_ref=stats_out, dst_ref=stats_in, send_sem=stats_sem.at[0], recv_sem=stats_sem.at[1],
        device_id=twin, device_id_type=MESH,
    )
    stats_copy.start()
    place_chunk(mine)
    stats_copy.wait()
    inverse = lax.rsqrt((power + stats_in[0:1, :]) / LAT + EPSILON)
    peak = jnp.maximum(
        jnp.maximum(latent_peak, stats_in[1:2, :]) * inverse,
        jnp.maximum(rope_peak, stats_in[2:3, :]),
    )
    scale = (peak + EPSILON).astype(jnp.bfloat16).astype(jnp.float32)

    def terms(value):
        found = []
        for _ in range(3):
            term = value.astype(jnp.bfloat16).astype(jnp.float32)
            found.append(term)
            value = value - term
        return found

    lines = terms(inverse / scale) + terms(1.0 / scale) + [scale]
    lines = lines + [jnp.zeros((SCALE_ROWS - len(lines), tokens), jnp.float32)]
    hand_over(jnp.concatenate(lines, axis=0).astype(jnp.bfloat16), 3, SCALE_ROWS)

    place_chunk(other)
    place_chunk(middle)

    slot_id = lax.broadcasted_iota(jnp.int32, (slot_total, 128), 0)
    lane = lax.broadcasted_iota(jnp.int32, (slot_total, 128), 1)
    for step in range(1, n_seq):
        source = (seq + step) % n_seq
        block_copy(source, source, 3, SCALE_ROWS).wait_recv()
    factors = jnp.concatenate(
        [incoming[source, cols : cols + SCALE_ROWS, :] for source in range(n_seq)], axis=1
    )
    by_row = lax.dot_general(placing[...], factors, NT, preferred_element_type=jnp.float32)
    latent_factor = by_row[:, 0:1] + by_row[:, 1:2] + by_row[:, 2:3]
    rope_factor = by_row[:, 3:4] + by_row[:, 4:5] + by_row[:, 5:6]
    column_id = lax.broadcasted_iota(jnp.int32, (1, cols), 1) + tp * cols
    factor = jnp.where(column_id < LAT, latent_factor, rope_factor)
    values = jnp.concatenate([in_slots[part] for part in range(3)], axis=1)
    cache_ref[...] = (values * factor).astype(jnp.bfloat16)
    placed = jnp.zeros((slot_total, 128), jnp.float32)
    for source in range(n_seq):
        low, high = slots[source]
        hit = slot_id == jnp.where(lane < 64, low, high)
        scales_in = incoming[source, cols : cols + SCALE_ROWS, :].astype(jnp.float32)
        placed = placed + jnp.where(hit, scales_in[6:7, :], 0.0)
    scales_ref[...] = (placed[:, :64] + placed[:, 64:]).astype(jnp.bfloat16)

    for step in range(1, n_seq):
        target = (seq + step) % n_seq
        for part in (mine, other, middle):
            block_copy(seq, target, part, chunk).wait_send()
        block_copy(seq, target, 3, SCALE_ROWS).wait_send()
    for part in (mine, middle):
        when_inside(z + 1, lambda: piece(own, part, 0, above, weight_hbm).wait_send())
        when_inside(z - 1, lambda: piece(own, part, 1, below, weight_hbm).wait_send())
        piece(own, part, 2, beside, weight_hbm).wait_send()

    def sent(z_from, x_from, direction, z_to, peer):
        def do():
            shard = z_from * X_COUNT + x_from
            for part in (mine, middle):
                if direction is not None:
                    when_inside(z_to, lambda: piece(shard, part, direction, peer).wait_send())
                    piece(shard, part, 2, beside).wait_send()
            piece(shard, mine, 3, across).wait_send()
        when_inside(z_from, do)

    sent(z, 1 - x, None, None, None)
    for distance in range(1, Z_COUNT):
        sent(z - distance, x, 0, z + 1, above)
        sent(z + distance, x, 1, z - 1, below)
        sent(z - distance, 1 - x, None, None, None)
        sent(z + distance, 1 - x, None, None, None)


def fused(hidden, in_gain, kv_weight, kv_gain, block_owner, block_slot):
    rows, width = hidden.shape
    depth, cols = kv_weight.shape
    n_seq = lax.axis_size("seq")
    tokens = 2 * rows
    slot_total = 2 * (tokens // 64)
    padded = cols + SCALE_ROWS
    vmem = pl.BlockSpec(memory_space=pltpu.VMEM)
    hbm = pl.BlockSpec(memory_space=pltpu.HBM)
    cache, scales = pl.pallas_call(
        fused_kernel,
        out_shape=(
            jax.ShapeDtypeStruct((slot_total * 64, cols), jnp.bfloat16),
            jax.ShapeDtypeStruct((slot_total, 64), jnp.bfloat16),
        ),
        in_specs=[hbm] * 6,
        out_specs=(vmem, vmem),
        scratch_shapes=[
            pltpu.SMEM(block_owner.shape, jnp.int32),
            pltpu.SMEM(block_slot.shape, jnp.int32),
            pltpu.VMEM((rows, width), jnp.bfloat16),
            pltpu.VMEM((width // 128, 128), jnp.bfloat16),
            pltpu.VMEM((LAT // 128, 128), jnp.bfloat16),
            pltpu.VMEM((8, width), jnp.float32),
            pltpu.SemaphoreType.DMA((6,)),
            pltpu.VMEM((n_seq, cols, depth), jnp.bfloat16),
            pltpu.VMEM((tokens, width), jnp.bfloat16),
            pltpu.VMEM((tokens, n_seq * 128), jnp.bfloat16),
            pltpu.VMEM((slot_total * 64, n_seq * 128), jnp.bfloat16),
            pltpu.VMEM((n_seq, padded, 128), jnp.bfloat16),
            pltpu.VMEM((n_seq, padded, 128), jnp.bfloat16),
            pltpu.VMEM((8, tokens), jnp.float32),
            pltpu.VMEM((8, tokens), jnp.float32),
            pltpu.VMEM((cols, 1), jnp.float32),
            pltpu.VMEM((3, slot_total * 64, cols // 3), jnp.float32),
            pltpu.SemaphoreType.DMA((n_seq, 3, 4)),
            pltpu.SemaphoreType.DMA((n_seq, 3)),
            pltpu.SemaphoreType.DMA((2,)),
            pltpu.SemaphoreType.DMA((2,)),
            pltpu.SemaphoreType.DMA((n_seq, 4)),
            pltpu.SemaphoreType.DMA((n_seq, 4)),
        ],
        compiler_params=pltpu.CompilerParams(
            collective_id=0, has_side_effects=True, vmem_limit_bytes=64 * 1024 * 1024 - 65536
        ),
    )(
        block_owner, block_slot, hidden, in_gain.reshape(width // 128, 128), kv_weight.T,
        kv_gain.reshape(LAT // 128, 128),
    )
    return (cache.reshape(slot_total, 64, cols), scales)


def solution(mesh):
    fits = (
        mesh.shape["seq"] == X_COUNT * Z_COUNT
        and mesh.shape["group"] == 2
        and mesh.shape["tp"] == 2
    )
    return jax.shard_map(
        fused if fits else per_device,
        mesh=mesh,
        in_specs=(P(("group", "seq", "tp"), None), P(), P("seq", "tp"), P(), P(), P()),
        out_specs=(P(("group", "seq"), None, "tp"), P(("group", "seq"), None)),
        check_vma=False,
    )
```
